128 devices in a mesh: dp: 8 (over y, core), mp: 16 (over z, x).
Axes of the slice: x: 4, y: 4, z: 4, core: 2. Of those that a mesh axis runs over, the one named last changes fastest.
Arguments:
- local_grads: bfloat16 [8, 64, 1024, 1024], P('dp', 'mp'), may hold values from -8 to 8
- left_root: bfloat16 [16, 8, 1024, 1024], P('mp', 'dp'), may hold values from -1 to 3
- right_root: bfloat16 [16, 8, 1024, 1024], P('mp', 'dp'), may hold values from -1 to 3
- accumulator: float32 [64, 1024, 1024], P('mp', 'dp'), may hold values from 0.5 to 5
- momentum: bfloat16 [64, 1024, 1024], P('mp', 'dp'), may hold values from -3 to 3
- block_owner: int32 [64], replicated, may hold values from 0 to 15, as said below
- block_slot: int32 [64], replicated, may hold values from 0 to 7, as said below
Outputs:
- new_accumulator: float32 [64, 1024, 1024], P('mp', 'dp')
- update: bfloat16 [64, 1024, 1024], P('mp')
The draws below stay inside these ranges and needn't reach their ends.
Inputs may be any that keep to these rules, and one draw needn't show every extreme that they name: `block_owner`: block m * 4 + j is block j of tensor-parallel shard m. The blocks of one shard have different owners. No owner holds more than 8 blocks, and some owner holds exactly 8. `block_slot`: two blocks with the same owner have different slots.
All inputs are finite; a program needn't handle non-finite values.
Results may differ from the reference program's by a relative error of at most 0.027.
Values may be sent and summed in bfloat16 or wider, within the bound.
A program may use at most 128 MiB of HBM per device.

```python
import math
import jax
import jax.numpy as jnp
from jax import lax

B = 1024
BLOCKS_DEV = 4
NBLK = 64
N_DP = 8
N_MP = 16


def owner_lookup_tables(seed_key):
    table_random_key = jax.random.fold_in(seed_key, 11)
    count_key, rotate_key, home_key, label_key = jax.random.split(table_random_key, 4)
    cell_total = (N_MP - 1) * N_DP
    chosen = jax.random.permutation(count_key, cell_total) < NBLK - N_DP
    counts_rest = jnp.sum(chosen.reshape(N_MP - 1, N_DP).astype(jnp.int32), axis=1)
    counts = jnp.concatenate([jnp.full((1,), N_DP, jnp.int32), counts_rest])
    group_ends = jnp.cumsum(counts).astype(jnp.int32)
    starts = group_ends - counts
    position = jnp.arange(NBLK, dtype=jnp.int32)
    grouped = jnp.sum((group_ends[None, :] <= position[:, None]).astype(jnp.int32), axis=1)
    start_of = starts[grouped]
    rotation = jax.random.randint(rotate_key, (N_MP,), 0, N_DP, dtype=jnp.int32)
    slot_sorted = (position - start_of + rotation[grouped]) % N_DP
    home_perm = jax.random.permutation(home_key, N_MP).astype(jnp.int32)
    label_perm = jax.random.permutation(label_key, N_MP).astype(jnp.int32)
    home_index = home_perm[position % N_MP]
    block_place = home_index * BLOCKS_DEV + position // N_MP
    owners = jnp.zeros((NBLK,), jnp.int32).at[block_place].set(label_perm[grouped])
    slots = jnp.zeros((NBLK,), jnp.int32).at[block_place].set(slot_sorted)
    return (owners, slots)


def draw_block_owner(key, part):
    owners, slots = owner_lookup_tables(key)
    return owners


def draw_block_slot(key, part):
    owners, slots = owner_lookup_tables(key)
    return slots


def draw_local_grads(key, part):
    key = jax.random.fold_in(key, 3)
    first_key = jax.random.fold_in(key, 0)
    jitter_key = jax.random.fold_in(key, 2)
    column_key = jax.random.fold_in(key, 3)
    full_shape = (N_DP, NBLK, B, B)
    base_draw = jax.random.truncated_normal(first_key, -4.0, 4.0, full_shape, jnp.float32)
    row_ramp = jnp.power(10.0, jnp.arange(B, dtype=jnp.float32) / B)
    jitter = jnp.exp(jax.random.uniform(jitter_key, (1, NBLK, B, 1), jnp.float32, 0.0, math.log(2.0)))
    columns = jnp.exp(jax.random.uniform(column_key, (1, NBLK, 1, B), jnp.float32, 0.0, math.log(10.0)))
    scaled_values = base_draw * (0.1 / math.sqrt(N_DP)) * row_ramp[None, None, :, None] * jitter * columns
    return jnp.clip(scaled_values, -8.0, 8.0).astype(jnp.bfloat16)


def factor_matrix(noise_part, diag_key, lowest, highest):
    symmetric = (noise_part + jnp.swapaxes(noise_part, 2, 3)) * (0.5 / math.sqrt(B))
    diagonal = jnp.exp(jax.random.uniform(diag_key, (N_MP, N_DP, B), jnp.float32, math.log(lowest), math.log(highest)))
    identity_mask = (jnp.arange(B)[:, None] == jnp.arange(B)[None, :]).astype(jnp.float32)
    return symmetric + identity_mask[None, None, :, :] * diagonal[:, :, :, None]


def draw_left_root(key, part):
    key = jax.random.fold_in(key, 5)
    noise_key, diag_key = jax.random.split(key)
    full_shape = (N_MP, N_DP, B, B)
    noise_part = jax.random.truncated_normal(noise_key, -4.0, 4.0, full_shape, jnp.float32)
    return factor_matrix(noise_part, diag_key, 0.5, 2.0).astype(jnp.bfloat16)


def draw_right_root(key, part):
    key = jax.random.fold_in(key, 7)
    noise_key, diag_key = jax.random.split(key)
    full_shape = (N_MP, N_DP, B, B)
    noise_part = jax.random.truncated_normal(noise_key, -4.0, 4.0, full_shape, jnp.float32)
    return factor_matrix(noise_part, diag_key, 0.5, 2.0).astype(jnp.bfloat16)


def block_scale(rng, dims, cuts, least, largest):
    def one(dim, blocks):
        steps = jax.random.uniform(jax.random.fold_in(jax.random.fold_in(rng, 6), dim), (blocks,), jnp.float32, least / len(cuts), largest / len(cuts))
        return jnp.repeat(jnp.exp(steps), dims[dim] // blocks).reshape((-1,) + (1,) * (len(dims) - dim - 1))

    level = one(*cuts[0])
    for cut in cuts[1:]:
        level = level * one(*cut)
    return level


def bell_draw(stream_key, dims, spread, bound, cuts=(), kind=jnp.bfloat16):
    loudness = block_scale(stream_key, dims, cuts, -0.22, 0.18) if cuts else 1.0
    values = jax.random.normal(stream_key, dims, jnp.float32) * spread * loudness
    return jnp.minimum(jnp.maximum(values, -bound), bound).astype(kind)


def setup_inputs(seed: int = 0) -> dict:
    seeds = jax.random.split(jax.random.key(seed), 8)
    return {
        "local_grads": draw_local_grads(jax.random.fold_in(seeds[7], 71), 0),
        "left_root": draw_left_root(jax.random.fold_in(seeds[7], 71), 0),
        "right_root": draw_right_root(jax.random.fold_in(seeds[7], 71), 0),
        "accumulator": jnp.clip(jnp.exp(math.log(5.0) - 2.3025851 * jax.random.uniform(seeds[3], (NBLK, B, B), jnp.float32) ** block_scale(seeds[3], (NBLK, B, B), ((0, 16), (1, 8)), -0.2, 0.2)), 0.5, 5.0),
        "momentum": bell_draw(seeds[4], (NBLK, B, B), 0.5, 3.0, ((0, 16), (1, 8))),
        "block_owner": draw_block_owner(jax.random.fold_in(seeds[7], 71), 0),
        "block_slot": draw_block_slot(jax.random.fold_in(seeds[7], 71), 0),
    }


beta_momentum = 0.9
eps_norm = 1e-06

def reference(local_grads, left_root, right_root, accumulator, momentum, block_owner, block_slot):

    def block_step(block_index):
        replica_grads = lax.dynamic_index_in_dim(local_grads, block_index, 1, keepdims=False)
        grad_sum = lax.optimization_barrier(jnp.sum(replica_grads.astype(jnp.float32), axis=0))
        accum_old = lax.dynamic_index_in_dim(accumulator, block_index, 0, keepdims=False)
        moment_old = lax.dynamic_index_in_dim(momentum, block_index, 0, keepdims=False)
        owner_here = block_owner[block_index]
        slot_here = block_slot[block_index]
        left_factor = left_root[owner_here, slot_here]
        right_factor = right_root[owner_here, slot_here]
        accum_new = accum_old + grad_sum * grad_sum
        adagrad = grad_sum * lax.rsqrt(accum_new)
        half_product = jnp.dot(grad_sum.astype(jnp.bfloat16), right_factor, preferred_element_type=jnp.float32).astype(jnp.bfloat16)
        precond = jnp.dot(left_factor, half_product, preferred_element_type=jnp.float32).astype(jnp.bfloat16)
        precond_wide = precond.astype(jnp.float32)
        graft_scale = jnp.sqrt(jnp.sum(adagrad * adagrad) / (jnp.sum(precond_wide * precond_wide) + eps_norm))
        moment_new = (beta_momentum * moment_old.astype(jnp.float32) + graft_scale * precond_wide).astype(jnp.bfloat16)
        return (accum_new, moment_new)
    new_accumulator, update = lax.map(block_step, jnp.arange(NBLK, dtype=jnp.int32))
    return (new_accumulator, update)
```

```python
import jax
import jax.numpy as jnp
from jax import lax
from jax.experimental import pallas as pl
from jax.experimental.pallas import tpu as pltpu
from jax.sharding import PartitionSpec as P

MESH = pl.DeviceIdType.MESH
BF = jnp.bfloat16
F32 = jnp.float32
beta_momentum = 0.9
eps_norm = 1e-06

CHUNKS = 4
ROWS = 32
W = 1024
COLUMN = ((1, 0), (3, 0), (2, 0), (1, 1), (3, 1), (2, 1), (0, 1))


def kernel(
    inv, loc, g, left, right, acc, mom, out_acc, out_upd,
    own, sib, t1p, t1m, t2p, t2m, accv, momv, lv, rv, ada, ar, sbuf, qb, p1, vb, gb, half, pp,
    nrm, nv, nt, nw, v2, wb, wp, hh, scl, up,
    s_own, s_in, s_sib, s_t1, s_t2, s_fa, s_fb, s_fc, s_ra, s_rb, s_rc, s_sm,
    s_a1, s_a2, s_sb, s_out, snd,
):
    dp = lax.axis_index("dp")
    mp = lax.axis_index("mp")
    y, c = dp // 2, dp % 2
    z, x = mp // 4, mp % 4
    piece_a, piece_h = mp // 8, mp % 8

    def col(dy, dc):
        return ((y + dy) % 4) * 2 + (c + dc) % 2

    def plane(k):
        return ((z + k // 4) % 4) * 4 + (x + k % 4) % 4

    def put(src, dst, ssem, rsem, device):
        pltpu.make_async_remote_copy(
            src_ref=src, dst_ref=dst, send_sem=snd.at[ssem], recv_sem=rsem,
            device_id=device, device_id_type=MESH,
        ).start()

    def keep(src, dst, sem):
        pltpu.make_async_copy(src, dst, sem).start()

    def await_bytes(ref, sem):
        pltpu.make_async_copy(ref, ref, sem).wait()

    def each_in_plane(body):
        def step(k, carry):
            body(plane(k))
            return carry

        lax.fori_loop(1, 16, step, 0)

    def piece(m):
        return pl.ds(pl.multiple_of((m // 8) * 16, 16), 16), pl.ds(
            pl.multiple_of((m % 8) * 128, 128), 128
        )

    up_dev = (col(1, 0), mp)
    down_dev = (col(3, 0), mp)
    sib_dev = (col(0, 1), mp)
    targets = ((y + 2) % 4, (y + 1) % 4, (y + 3) % 4, y)

    for q in range(CHUNKS):
        for k in range(4):
            keep(
                g.at[:, targets[k], c, pl.ds(q * ROWS, ROWS), :],
                own.at[q, targets[k]],
                s_own.at[q * 4 + k],
            )
    keep(acc, accv, s_in.at[0])
    keep(right, rv, s_in.at[1])
    keep(left, lv, s_in.at[2])
    keep(mom, momv, s_in.at[3])

    barrier = pltpu.get_barrier_semaphore()

    def greet(m):
        pl.semaphore_signal(barrier, inc=1, device_id=(dp, m), device_id_type=MESH)

    for dy, dc in COLUMN:
        pl.semaphore_signal(barrier, inc=1, device_id=(col(dy, dc), mp), device_id_type=MESH)
    each_in_plane(greet)
    pl.semaphore_wait(barrier, 22)

    for q in range(CHUNKS):
        for k in range(4):
            put(
                g.at[:, targets[k], 1 - c, pl.ds(q * ROWS, ROWS), :],
                sib.at[q, targets[k]],
                0,
                s_sib.at[q * 4 + k],
                sib_dev,
            )

    for j in range(4):
        ada[j] = jnp.zeros((8, 128), F32)

    def both(q, k, j):
        t = targets[k]
        return own[q, t, j].astype(F32) + sib[q, t, j].astype(F32)

    def arrived(q, k):
        await_bytes(own.at[q, targets[k]], s_own.at[q * 4 + k])
        await_bytes(sib.at[q, targets[k]], s_sib.at[q * 4 + k])

    def fold(v):
        rows, lanes = v.shape
        v = jnp.sum(v.reshape(rows // 8, 8, lanes), axis=0)
        total = v[:, 0:128]
        for i in range(1, lanes // 128):
            total = total + v[:, i * 128 : (i + 1) * 128]
        return total

    def f0(q):
        arrived(q, 0)
        t = targets[0]
        for j in range(4):
            own[q, t, j] = both(q, 0, j).astype(BF)
        put(own.at[q, t, pl.ds(0, 2)], t1p.at[q], 1, s_t1.at[q * 2], up_dev)
        put(own.at[q, t, pl.ds(2, 2)], t1m.at[q], 1, s_t1.at[q * 2 + 1], down_dev)

    def f1(q):
        arrived(q, 1)
        arrived(q, 2)
        await_bytes(t1p.at[q], s_t1.at[q * 2])
        await_bytes(t1m.at[q], s_t1.at[q * 2 + 1])
        for j in range(4):
            value = both(q, 1, j)
            if j < 2:
                value = value + t1p[q, j].astype(F32)
            own[q, targets[1], j] = value.astype(BF)
        put(own.at[q, targets[1]], t2p.at[q], 2, s_t2.at[q * 2], up_dev)
        for j in range(4):
            value = both(q, 2, j)
            if j >= 2:
                value = value + t1m[q, j - 2].astype(F32)
            own[q, targets[2], j] = value.astype(BF)
        put(own.at[q, targets[2]], t2m.at[q], 2, s_t2.at[q * 2 + 1], down_dev)

    def f2(q):
        arrived(q, 3)
        await_bytes(t2p.at[q], s_t2.at[q * 2])
        await_bytes(t2m.at[q], s_t2.at[q * 2 + 1])
        if q == 0:
            await_bytes(accv, s_in.at[0])
        rows = pl.ds(q * ROWS, ROWS)
        for j in range(4):
            total = both(q, 3, j) + t2p[q, j].astype(F32) + t2m[q, j].astype(F32)
            fresh = accv[j, rows, :] + total * total
            accv[j, rows, :] = fresh
            step = total * lax.rsqrt(fresh)
            ada[j] += fold(step * step)
            sbuf[q, j] = total.astype(BF)
        keep(accv.at[:, rows, :], out_acc.at[:, rows, :], s_out.at[q])

        def spread(m):
            r, l = piece(m)
            put(sbuf.at[q, :, r, l], qb[q].at[pl.ds(mp * 4, 4)], 3, s_fa.at[q], (dp, m))

        each_in_plane(spread)
        r, l = piece(mp)
        keep(sbuf.at[q, :, r, l], qb[q].at[pl.ds(mp * 4, 4)], s_fa.at[q])

    def share_adagrad():
        ar[dp] = ada[...]
        for dy, dc in COLUMN:
            put(ada, ar.at[dp], 4, s_sm.at[0], (col(dy, dc), mp))

    def f3(q):
        await_bytes(qb[q], s_fa.at[q])

        def pick(i, carry):
            for n in range(8):
                p1[q, i * 8 + n] = qb[q][inv[i * 8 + n]]
            return carry

        lax.fori_loop(0, 16, pick, 0)
        r, l = piece(mp)

        def deal(o):
            put(p1.at[q, pl.ds(o * 8, 8)], vb.at[q, :, r, l], 5, s_fb.at[q], (dp, o))

        each_in_plane(deal)
        keep(p1.at[q, pl.ds(mp * 8, 8)], vb.at[q, :, r, l], s_fb.at[q])

    def f4(q):
        await_bytes(vb.at[q], s_fb.at[q])
        for dy, dc in COLUMN:
            s = col(dy, dc)
            put(vb.at[q, s], gb.at[q, dp], 6, s_fc.at[q], (s, mp))
        keep(vb.at[q, dp], gb.at[q, dp], s_fc.at[q])

    def f5(q):
        if q == 0:
            await_bytes(rv, s_in.at[1])
        await_bytes(gb.at[q], s_fc.at[q])

        def tile(n, carry):
            lanes = pl.ds(pl.multiple_of(n * 256, 256), 256)
            rows = gb[q].reshape(8 * ROWS, W)
            value = jnp.dot(rows, rv[:, lanes], preferred_element_type=F32)
            half[:, pl.ds(q * ROWS, ROWS), lanes] = value.astype(BF).reshape(8, ROWS, 256)
            return carry

        lax.fori_loop(0, 4, tile, 0)

    def r0(q):
        if q == 0:
            await_bytes(lv, s_in.at[2])
            nrm[...] = jnp.zeros((8, 128), F32)

        def tile(n, carry):
            lanes = pl.ds(pl.multiple_of(n * 256, 256), 256)
            rows = lv[:, pl.ds(q * ROWS, ROWS), :].reshape(8 * ROWS, W)
            value = jnp.dot(rows, half[:, :, lanes].reshape(W, 256), preferred_element_type=F32)
            value = value.astype(BF)
            pp[q, :, :, lanes] = value.reshape(8, ROWS, 256)
            wide = value.astype(F32)
            nrm[...] += fold(wide * wide)
            return carry

        lax.fori_loop(0, 4, tile, 0)
        for dy, dc in COLUMN:
            d = col(dy, dc)
            put(pp.at[q, d], v2.at[q, dp], 7, s_ra.at[q], (d, mp))
        keep(pp.at[q, dp], v2.at[q, dp], s_ra.at[q])

    def share_norm():
        total = jnp.full((8, 128), jnp.sum(nrm[...]), F32)
        nrm[...] = total
        nv[dp] = total
        for dy, dc in COLUMN:
            put(nrm, nv.at[dp], 8, s_sm.at[1], (col(dy, dc), mp))

    def spread_norms():
        await_bytes(nv.at[pl.ds(0, 7)], s_sm.at[1])
        row = lax.broadcasted_iota(jnp.int32, (8, 128), 0)
        table = jnp.zeros((8, 128), F32)
        for s in range(8):
            table = jnp.where(row == s, nv[s], table)
        nt[...] = table
        nw[mp] = table

        def send(m):
            put(nt, nw.at[mp], 9, s_sm.at[2], (dp, m))

        each_in_plane(send)

    def r1(q):
        await_bytes(v2.at[q], s_ra.at[q])

        def spread(m):
            r, l = piece(m)
            put(v2.at[q, :, r, l], wb[q].at[pl.ds(mp * 8, 8)], 10, s_rb.at[q], (dp, m))

        each_in_plane(spread)
        r, l = piece(mp)
        keep(v2.at[q, :, r, l], wb[q].at[pl.ds(mp * 8, 8)], s_rb.at[q])

    def r2(q):
        await_bytes(wb[q], s_rb.at[q])

        def pick(i, carry):
            for n in range(8):
                wp[q, i * 8 + n] = wb[q][loc[i * 8 + n]]
            return carry

        lax.fori_loop(0, 8, pick, 0)
        r, l = piece(mp)

        def deal(m):
            put(wp.at[q, pl.ds(m * 4, 4)], hh.at[q, :, r, l], 11, s_rc.at[q], (dp, m))

        each_in_plane(deal)
        keep(wp.at[q, pl.ds(mp * 4, 4)], hh.at[q, :, r, l], s_rc.at[q])

    def scales():
        await_bytes(ar.at[pl.ds(0, 7)], s_sm.at[0])
        await_bytes(nw.at[pl.ds(0, 15)], s_sm.at[2])
        await_bytes(momv, s_in.at[3])
        row = lax.broadcasted_iota(jnp.int32, (8, 128), 0)
        for j in range(4):
            place = loc[mp * 4 + j]
            mine = nw[place // 8]
            pre = jnp.sum(jnp.where(row == place % 8, mine, 0.0), axis=0, keepdims=True)
            ada_total = jnp.sum(ar[:, j])
            scl[j] = jnp.broadcast_to(jnp.sqrt(ada_total / (pre + eps_norm)), (8, 128))

    def group(dy):
        return col(dy, 0)

    def rows_of(dy, q, blocks=None):
        if blocks is None:
            return out_upd.at[:, group(dy), pl.ds(q * ROWS, ROWS), :]
        return out_upd.at[pl.ds(blocks, 2), group(dy), pl.ds(q * ROWS, ROWS), :]

    def r3(q):
        await_bytes(hh.at[q], s_rc.at[q])
        for j in range(4):
            scale = jnp.concatenate([scl[j, 0:1, :]] * 8, axis=1)
            value = (
                beta_momentum * momv[j, pl.ds(q * ROWS, ROWS), :].astype(F32)
                + scale * hh[q, j].astype(F32)
            )
            up[q, j] = value.astype(BF)
        put(up.at[q], rows_of(0, q), 12, s_a1.at[q * 2], up_dev)
        put(up.at[q], rows_of(0, q), 12, s_a1.at[q * 2 + 1], down_dev)
        put(up.at[q], rows_of(0, q), 14, s_sb.at[q * 4], sib_dev)
        keep(up.at[q], rows_of(0, q), s_out.at[4 + q])

    def r4(q):
        await_bytes(rows_of(3, q), s_a1.at[q * 2])
        put(rows_of(3, q, 0), rows_of(3, q, 0), 13, s_a2.at[q * 2], up_dev)
        put(rows_of(3, q), rows_of(3, q), 14, s_sb.at[q * 4 + 1], sib_dev)
        await_bytes(rows_of(1, q), s_a1.at[q * 2 + 1])
        put(rows_of(1, q, 2), rows_of(1, q, 2), 13, s_a2.at[q * 2 + 1], down_dev)
        put(rows_of(1, q), rows_of(1, q), 14, s_sb.at[q * 4 + 2], sib_dev)

    def r5(q):
        await_bytes(rows_of(2, q, 0), s_a2.at[q * 2])
        await_bytes(rows_of(2, q, 2), s_a2.at[q * 2 + 1])
        put(rows_of(2, q), rows_of(2, q), 14, s_sb.at[q * 4 + 3], sib_dev)

    forward = (f0, f1, f2, f3, f4, f5)
    for t in range(CHUNKS + len(forward) - 1):
        for n, stage in enumerate(forward):
            if 0 <= t - n < CHUNKS:
                stage(t - n)
        if t == CHUNKS + 1:
            share_adagrad()
    for q in range(CHUNKS):
        r0(q)
    share_norm()
    back = (r1, r2, r3, r4, r5)
    for t in range(CHUNKS + len(back) - 1):
        if t == 1:
            spread_norms()
        if t == 2:
            scales()
        for n, stage in enumerate(back):
            if 0 <= t - n < CHUNKS:
                stage(t - n)

    for q in range(CHUNKS):
        for k in range(4):
            await_bytes(rows_of((0, 3, 1, 2)[k], q), s_sb.at[q * 4 + k])
        rows = pl.ds(q * ROWS, ROWS)
        await_bytes(out_acc.at[:, rows, :], s_out.at[q])
        await_bytes(rows_of(0, q), s_out.at[4 + q])
        for k in range(4):
            await_bytes(sib.at[q, k], snd.at[0])
            await_bytes(rows_of(k, q), snd.at[14])
        await_bytes(t1p.at[q], snd.at[1])
        await_bytes(t1m.at[q], snd.at[1])
        await_bytes(t2p.at[q], snd.at[2])
        await_bytes(t2m.at[q], snd.at[2])
        await_bytes(qb[q].at[pl.ds(0, 60)], snd.at[3])
        await_bytes(p1.at[q, pl.ds(0, 120)], snd.at[5])
        await_bytes(vb.at[q, pl.ds(0, 7)], snd.at[6])
        await_bytes(pp.at[q, pl.ds(0, 7)], snd.at[7])
        await_bytes(wb[q].at[pl.ds(0, 120)], snd.at[10])
        await_bytes(wp.at[q, pl.ds(0, 60)], snd.at[11])
        await_bytes(rows_of(1, q), snd.at[12])
        await_bytes(rows_of(3, q), snd.at[12])
        await_bytes(rows_of(2, q), snd.at[13])
    await_bytes(ar.at[pl.ds(0, 7)], snd.at[4])
    await_bytes(nv.at[pl.ds(0, 7)], snd.at[8])
    await_bytes(nw.at[pl.ds(0, 15)], snd.at[9])


def shards(local_grads, left_root, right_root, accumulator, momentum, block_owner, block_slot):
    place = block_owner * 8 + block_slot
    hit = place[None, :] == jnp.arange(128, dtype=jnp.int32)[:, None]
    inverse = jnp.sum(
        jnp.where(hit, jnp.arange(64, dtype=jnp.int32)[None, :], 0), axis=1, dtype=jnp.int32
    )
    hbm = pl.BlockSpec(memory_space=pl.ANY)
    smem = pl.BlockSpec(memory_space=pltpu.SMEM)
    V = pltpu.VMEM
    dma = pltpu.SemaphoreType.DMA
    C, R = CHUNKS, ROWS
    scratch = [
        V((C, 4, 4, R, W), BF), V((C, 4, 4, R, W), BF),
        V((C, 2, R, W), BF), V((C, 2, R, W), BF),
        V((C, 4, R, W), BF), V((C, 4, R, W), BF),
        V((4, 128, W), F32), V((4, 128, W), BF),
        V((8, 128, W), BF), V((W, W), BF),
        V((4, 8, 128), F32), V((8, 4, 8, 128), F32),
        V((C, 4, R, W), BF),
        [V((64, 16, 128), BF)] * C, V((C, 128, 16, 128), BF),
        V((C, 8, R, W), BF), V((C, 8, R, W), BF),
        V((8, 128, W), BF), V((C, 8, R, W), BF),
        V((8, 128), F32), V((8, 8, 128), F32),
        V((8, 128), F32), V((16, 8, 128), F32),
        V((C, 8, R, W), BF),
        [V((128, 16, 128), BF)] * C, V((C, 64, 16, 128), BF),
        V((C, 4, R, W), BF), V((4, 8, 128), F32), V((C, 4, R, W), BF),
        dma((16,)), dma((4,)), dma((16,)), dma((8,)), dma((8,)),
        dma((4,)), dma((4,)), dma((4,)), dma((4,)), dma((4,)), dma((4,)),
        dma((3,)), dma((8,)), dma((8,)), dma((16,)), dma((8,)), dma((15,)),
    ]
    accum_new, update = pl.pallas_call(
        kernel,
        out_shape=(
            jax.ShapeDtypeStruct((4, 128, W), F32),
            jax.ShapeDtypeStruct((4, 8, 128, W), BF),
        ),
        in_specs=[smem, smem] + [hbm] * 5,
        out_specs=(hbm, hbm),
        scratch_shapes=scratch,
        name="shampoo_step",
        compiler_params=pltpu.CompilerParams(
            collective_id=0, has_side_effects=True, vmem_limit_bytes=56 * 2**20
        ),
    )(
        inverse,
        place,
        local_grads.reshape(4, 4, 2, 128, W),
        left_root.reshape(8, 128, W),
        right_root.reshape(W, W),
        accumulator,
        momentum,
    )
    return accum_new, update.reshape(4, W, W)


def solution(mesh):
    placed = (
        P("dp", "mp", None, None),
        P("mp", "dp", None, None),
        P("mp", "dp", None, None),
        P("mp", "dp", None),
        P("mp", "dp", None),
        P(),
        P(),
    )
    return jax.shard_map(
        shards,
        mesh=mesh,
        in_specs=placed,
        out_specs=(P("mp", "dp", None), P("mp", None, None)),
        check_vma=False,
    )
```

```python
import jax
import jax.numpy as jnp
from jax import lax
from jax.experimental import pallas as pl
from jax.experimental.pallas import tpu as pltpu
from jax.sharding import PartitionSpec as P

MESH = pl.DeviceIdType.MESH
BF = jnp.bfloat16
F32 = jnp.float32
beta_momentum = 0.9
eps_norm = 1e-06

CHUNKS = 4
ROWS = 32
W = 1024
COLUMN = ((2, 0), (2, 1), (1, 0), (3, 0), (1, 1), (3, 1), (0, 1))
PLANE = (
    (2, 2), (1, 2), (2, 1), (3, 2), (2, 3), (0, 2), (2, 0), (1, 1),
    (3, 3), (1, 3), (3, 1), (0, 1), (1, 0), (0, 3), (3, 0),
)


def kernel(
    owner, slot, g, left, right, acc, mom, out_acc, out_upd,
    own, sib, t1p, t1m, t2p, t2m, accv, momv, lv, rv, ada, ar, sbuf, qb, p1, vb, gb, half, pp,
    nrm, nv, nt, nw, v2, wb, wp, hh, scl, up, invv, inv,
    s_own, s_in, s_sib, s_t1, s_t2, s_fa, s_fb, s_fc, s_ra, s_rb, s_rc, s_sm,
    s_a1, s_a2, s_sb, s_out, s_inv, snd,
):
    dp = lax.axis_index("dp")
    mp = lax.axis_index("mp")
    y, c = dp // 2, dp % 2
    z, x = mp // 4, mp % 4
    piece_a, piece_h = mp // 8, mp % 8

    def col(dy, dc):
        return ((y + dy) % 4) * 2 + (c + dc) % 2

    def plane(dz, dx):
        return ((z + dz) % 4) * 4 + (x + dx) % 4

    def put(src, dst, ssem, rsem, device):
        pltpu.make_async_remote_copy(
            src_ref=src, dst_ref=dst, send_sem=snd.at[ssem], recv_sem=rsem,
            device_id=device, device_id_type=MESH,
        ).start()

    def keep(src, dst, sem):
        pltpu.make_async_copy(src, dst, sem).start()

    def await_bytes(ref, sem):
        pltpu.make_async_copy(ref, ref, sem).wait()

    ends = []

    def place(b):
        return owner[b] * 8 + slot[b]

    def each_in_plane(body):
        for dz, dx in PLANE:
            body(plane(dz, dx))

    def piece(m):
        return pl.ds(pl.multiple_of((m // 8) * 16, 16), 16), pl.ds(
            pl.multiple_of((m % 8) * 128, 128), 128
        )

    up_dev = (col(1, 0), mp)
    down_dev = (col(3, 0), mp)
    sib_dev = (col(0, 1), mp)
    targets = ((y + 2) % 4, (y + 1) % 4, (y + 3) % 4, y)

    barrier = pltpu.get_barrier_semaphore()

    def greet(m):
        pl.semaphore_signal(barrier, inc=1, device_id=(dp, m), device_id_type=MESH)

    for dy, dc in COLUMN:
        pl.semaphore_signal(barrier, inc=1, device_id=(col(dy, dc), mp), device_id_type=MESH)
    each_in_plane(greet)
    for q in range(CHUNKS):
        for k in range(4):
            keep(
                g.at[:, targets[k], c, pl.ds(q * ROWS, ROWS), :],
                own.at[q, targets[k]],
                s_own.at[q * 4 + k],
            )
    lane = lax.broadcasted_iota(jnp.int32, (8, 128), 1)

    def fill(b, table):
        return jnp.where(lane == place(b), b, table)

    invv[...] = lax.fori_loop(0, 64, fill, jnp.zeros((8, 128), jnp.int32))
    keep(invv, inv, s_inv.at[0])
    keep(acc, accv, s_in.at[0])
    keep(right, rv, s_in.at[1])
    keep(left, lv, s_in.at[2])
    keep(mom, momv, s_in.at[3])

    pl.semaphore_wait(barrier, 22)

    def swap(q):
        for k in range(4):
            put(
                g.at[:, targets[k], 1 - c, pl.ds(q * ROWS, ROWS), :],
                sib.at[q, targets[k]],
                0,
                s_sib.at[q * 4 + k],
                sib_dev,
            )
            ends.append((sib.at[q, k], snd.at[0]))

    for j in range(4):
        ada[j] = jnp.zeros((8, 128), F32)

    def both(q, k, j):
        t = targets[k]
        return own[q, t, j].astype(F32) + sib[q, t, j].astype(F32)

    def arrived(q, k):
        await_bytes(own.at[q, targets[k]], s_own.at[q * 4 + k])
        await_bytes(sib.at[q, targets[k]], s_sib.at[q * 4 + k])

    def fold(v):
        rows, lanes = v.shape
        v = jnp.sum(v.reshape(rows // 8, 8, lanes), axis=0)
        total = v[:, 0:128]
        for i in range(1, lanes // 128):
            total = total + v[:, i * 128 : (i + 1) * 128]
        return total

    def f0(q):
        if q + 1 < CHUNKS:
            swap(q + 1)
        arrived(q, 0)
        t = targets[0]
        for j in range(4):
            own[q, t, j] = both(q, 0, j).astype(BF)
        put(own.at[q, t, pl.ds(0, 2)], t1p.at[q], 1, s_t1.at[q * 2], up_dev)
        put(own.at[q, t, pl.ds(2, 2)], t1m.at[q], 1, s_t1.at[q * 2 + 1], down_dev)
        ends.extend([(t1p.at[q], snd.at[1]), (t1m.at[q], snd.at[1])])

    def f1(q):
        arrived(q, 1)
        arrived(q, 2)
        await_bytes(t1p.at[q], s_t1.at[q * 2])
        await_bytes(t1m.at[q], s_t1.at[q * 2 + 1])
        for j in range(4):
            value = both(q, 1, j)
            if j < 2:
                value = value + t1p[q, j].astype(F32)
            own[q, targets[1], j] = value.astype(BF)
        put(own.at[q, targets[1]], t2p.at[q], 2, s_t2.at[q * 2], up_dev)
        for j in range(4):
            value = both(q, 2, j)
            if j >= 2:
                value = value + t1m[q, j - 2].astype(F32)
            own[q, targets[2], j] = value.astype(BF)
        put(own.at[q, targets[2]], t2m.at[q], 2, s_t2.at[q * 2 + 1], down_dev)
        ends.extend([(t2p.at[q], snd.at[2]), (t2m.at[q], snd.at[2])])

    def f2(q):
        arrived(q, 3)
        await_bytes(t2p.at[q], s_t2.at[q * 2])
        await_bytes(t2m.at[q], s_t2.at[q * 2 + 1])
        if q == 0:
            await_bytes(accv, s_in.at[0])
        rows = pl.ds(q * ROWS, ROWS)
        for j in range(4):
            total = both(q, 3, j) + t2p[q, j].astype(F32) + t2m[q, j].astype(F32)
            fresh = accv[j, rows, :] + total * total
            accv[j, rows, :] = fresh
            step = total * lax.rsqrt(fresh)
            ada[j] += fold(step * step)
            sbuf[q, j] = total.astype(BF)
        keep(accv.at[:, rows, :], out_acc.at[:, rows, :], s_out.at[q])

        def spread(m):
            r, l = piece(m)
            put(sbuf.at[q, :, r, l], qb[q].at[pl.ds(mp * 4, 4)], 3, s_fa.at[q], (dp, m))

        each_in_plane(spread)
        r, l = piece(mp)
        keep(sbuf.at[q, :, r, l], qb[q].at[pl.ds(mp * 4, 4)], s_fa.at[q])
        ends.extend([(qb[q].at[pl.ds(0, 60)], snd.at[3]), (out_acc.at[:, rows, :], s_out.at[q])])

    def share_adagrad():
        ar[dp] = ada[...]
        for dy, dc in COLUMN:
            put(ada, ar.at[dp], 4, s_sm.at[0], (col(dy, dc), mp))
        ends.append((ar.at[pl.ds(0, 7)], snd.at[4]))

    def f3(q):
        if q == 0:
            await_bytes(invv, s_inv.at[0])
        await_bytes(qb[q], s_fa.at[q])

        def pick(i, carry):
            for n in range(8):
                p1[q, i * 8 + n] = qb[q][inv[0, i * 8 + n]]
            return carry

        lax.fori_loop(0, 16, pick, 0)
        r, l = piece(mp)

        def deal(o):
            put(p1.at[q, pl.ds(o * 8, 8)], vb.at[q, :, r, l], 5, s_fb.at[q], (dp, o))

        each_in_plane(deal)
        keep(p1.at[q, pl.ds(mp * 8, 8)], vb.at[q, :, r, l], s_fb.at[q])
        ends.append((p1.at[q, pl.ds(0, 120)], snd.at[5]))

    def f4(q):
        await_bytes(vb.at[q], s_fb.at[q])
        for dy, dc in COLUMN:
            s = col(dy, dc)
            put(vb.at[q, s], gb.at[q, dp], 6, s_fc.at[q], (s, mp))
        keep(vb.at[q, dp], gb.at[q, dp], s_fc.at[q])
        ends.append((vb.at[q, pl.ds(0, 7)], snd.at[6]))

    def f5(q):
        if q == 0:
            await_bytes(rv, s_in.at[1])
        await_bytes(gb.at[q], s_fc.at[q])

        def tile(n, carry):
            lanes = pl.ds(pl.multiple_of(n * 256, 256), 256)
            rows = gb[q].reshape(8 * ROWS, W)
            value = jnp.dot(rows, rv[:, lanes], preferred_element_type=F32)
            half[:, pl.ds(q * ROWS, ROWS), lanes] = value.astype(BF).reshape(8, ROWS, 256)
            return carry

        lax.fori_loop(0, 4, tile, 0)

    def product(q):
        if q == 0:
            await_bytes(lv, s_in.at[2])
            nrm[...] = jnp.zeros((8, 128), F32)

        def tile(n, carry):
            lanes = pl.ds(pl.multiple_of(n * 256, 256), 256)
            rows = lv[:, pl.ds(q * ROWS, ROWS), :].reshape(8 * ROWS, W)
            value = jnp.dot(rows, half[:, :, lanes].reshape(W, 256), preferred_element_type=F32)
            value = value.astype(BF)
            pp[q, :, :, lanes] = value.reshape(8, ROWS, 256)
            wide = value.astype(F32)
            nrm[...] += fold(wide * wide)
            return carry

        lax.fori_loop(0, 4, tile, 0)

    def r0(q):
        for dy, dc in COLUMN:
            d = col(dy, dc)
            put(pp.at[q, d], v2.at[q, dp], 7, s_ra.at[q], (d, mp))
        keep(pp.at[q, dp], v2.at[q, dp], s_ra.at[q])
        ends.append((pp.at[q, pl.ds(0, 7)], snd.at[7]))

    def share_norm():
        total = jnp.full((8, 128), jnp.sum(nrm[...]), F32)
        nrm[...] = total
        nv[dp] = total
        for dy, dc in COLUMN:
            put(nrm, nv.at[dp], 8, s_sm.at[1], (col(dy, dc), mp))
        ends.append((nv.at[pl.ds(0, 7)], snd.at[8]))

    def spread_norms():
        await_bytes(nv.at[pl.ds(0, 7)], s_sm.at[1])
        row = lax.broadcasted_iota(jnp.int32, (8, 128), 0)
        table = jnp.zeros((8, 128), F32)
        for s in range(8):
            table = jnp.where(row == s, nv[s], table)
        nt[...] = table
        nw[mp] = table

        def send(m):
            put(nt, nw.at[mp], 9, s_sm.at[2], (dp, m))

        each_in_plane(send)
        ends.append((nw.at[pl.ds(0, 15)], snd.at[9]))

    def r1(q):
        await_bytes(v2.at[q], s_ra.at[q])

        def spread(m):
            r, l = piece(m)
            put(v2.at[q, :, r, l], wb[q].at[pl.ds(mp * 8, 8)], 10, s_rb.at[q], (dp, m))

        each_in_plane(spread)
        r, l = piece(mp)
        keep(v2.at[q, :, r, l], wb[q].at[pl.ds(mp * 8, 8)], s_rb.at[q])
        ends.append((wb[q].at[pl.ds(0, 120)], snd.at[10]))

    def r2(q):
        await_bytes(wb[q], s_rb.at[q])

        def pick(i, carry):
            for n in range(8):
                wp[q, i * 8 + n] = wb[q][place(i * 8 + n)]
            return carry

        lax.fori_loop(0, 8, pick, 0)
        r, l = piece(mp)

        def deal(m):
            put(wp.at[q, pl.ds(m * 4, 4)], hh.at[q, :, r, l], 11, s_rc.at[q], (dp, m))

        each_in_plane(deal)
        keep(wp.at[q, pl.ds(mp * 4, 4)], hh.at[q, :, r, l], s_rc.at[q])
        ends.append((wp.at[q, pl.ds(0, 60)], snd.at[11]))

    def scales():
        await_bytes(ar.at[pl.ds(0, 7)], s_sm.at[0])
        await_bytes(nw.at[pl.ds(0, 15)], s_sm.at[2])
        await_bytes(momv, s_in.at[3])
        row = lax.broadcasted_iota(jnp.int32, (8, 128), 0)
        for j in range(4):
            mine = nw[owner[mp * 4 + j]]
            pre = jnp.sum(jnp.where(row == slot[mp * 4 + j], mine, 0.0), axis=0, keepdims=True)
            ada_total = jnp.sum(ar[:, j])
            scl[j] = jnp.broadcast_to(jnp.sqrt(ada_total / (pre + eps_norm)), (8, 128))

    def group(dy):
        return col(dy, 0)

    def rows_of(dy, q, blocks=None):
        if blocks is None:
            return out_upd.at[:, group(dy), pl.ds(q * ROWS, ROWS), :]
        return out_upd.at[pl.ds(blocks, 2), group(dy), pl.ds(q * ROWS, ROWS), :]

    def r3(q):
        await_bytes(hh.at[q], s_rc.at[q])
        for j in range(4):
            scale = jnp.concatenate([scl[j, 0:1, :]] * 8, axis=1)
            value = (
                beta_momentum * momv[j, pl.ds(q * ROWS, ROWS), :].astype(F32)
                + scale * hh[q, j].astype(F32)
            )
            up[q, j] = value.astype(BF)
        put(up.at[q], rows_of(0, q), 12, s_a1.at[q * 2], up_dev)
        put(up.at[q], rows_of(0, q), 12, s_a1.at[q * 2 + 1], down_dev)
        put(up.at[q], rows_of(0, q), 14, s_sb.at[q * 4], sib_dev)
        keep(up.at[q], rows_of(0, q), s_out.at[4 + q])
        for k in (1, 3):
            ends.append((rows_of(k, q), snd.at[12]))
        ends.extend([(rows_of(0, q), snd.at[14]), (rows_of(0, q), s_out.at[4 + q])])
        ends.append((rows_of(0, q), s_sb.at[q * 4]))

    def r4(q):
        await_bytes(rows_of(3, q), s_a1.at[q * 2])
        put(rows_of(3, q, 0), rows_of(3, q, 0), 13, s_a2.at[q * 2], up_dev)
        put(rows_of(3, q), rows_of(3, q), 14, s_sb.at[q * 4 + 1], sib_dev)
        await_bytes(rows_of(1, q), s_a1.at[q * 2 + 1])
        put(rows_of(1, q, 2), rows_of(1, q, 2), 13, s_a2.at[q * 2 + 1], down_dev)
        put(rows_of(1, q), rows_of(1, q), 14, s_sb.at[q * 4 + 2], sib_dev)
        ends.append((rows_of(2, q), snd.at[13]))
        for k in (1, 3):
            ends.append((rows_of(k, q), snd.at[14]))
        ends.extend([(rows_of(3, q), s_sb.at[q * 4 + 1]), (rows_of(1, q), s_sb.at[q * 4 + 2])])

    def r5(q):
        await_bytes(rows_of(2, q, 0), s_a2.at[q * 2])
        await_bytes(rows_of(2, q, 2), s_a2.at[q * 2 + 1])
        put(rows_of(2, q), rows_of(2, q), 14, s_sb.at[q * 4 + 3], sib_dev)
        ends.extend([(rows_of(2, q), snd.at[14]), (rows_of(2, q), s_sb.at[q * 4 + 3])])

    swap(0)
    forward = (f0, f1, f2, f3, f4, f5)
    for t in range(CHUNKS + len(forward) - 1):
        for n, stage in enumerate(forward):
            if 0 <= t - n < CHUNKS:
                stage(t - n)
        if t == CHUNKS + 1:
            share_adagrad()
    product(0)
    r0(0)
    for q in range(1, CHUNKS):
        product(q)
    share_norm()
    back = (r0, r1, r2, r3, r4, r5)
    for t in range(1, CHUNKS + len(back) - 1):
        if t == 2:
            spread_norms()
        if t == 3:
            scales()
        for n, stage in enumerate(back):
            if 0 <= t - n < CHUNKS:
                stage(t - n)

    for ref, sem in ends:
        await_bytes(ref, sem)


def store(acc, upd, out_acc, out_upd, sems):
    copies = []
    for j in range(4):
        copies.append(pltpu.make_async_copy(acc.at[j], out_acc.at[j], sems.at[j]))
        copies.append(pltpu.make_async_copy(upd.at[j], out_upd.at[j], sems.at[4 + j]))
    for copy in copies:
        copy.start()
    for copy in copies:
        copy.wait()


def shards(local_grads, left_root, right_root, accumulator, momentum, block_owner, block_slot):
    hbm = pl.BlockSpec(memory_space=pl.ANY)
    vmem = pl.BlockSpec(memory_space=pltpu.VMEM)
    smem = pl.BlockSpec(memory_space=pltpu.SMEM)
    V = pltpu.VMEM
    dma = pltpu.SemaphoreType.DMA
    C, R = CHUNKS, ROWS
    scratch = [
        V((C, 4, 4, R, W), BF), V((C, 4, 4, R, W), BF),
        V((C, 2, R, W), BF), V((C, 2, R, W), BF),
        V((C, 4, R, W), BF), V((C, 4, R, W), BF),
        V((4, 128, W), F32), V((4, 128, W), BF),
        V((8, 128, W), BF), V((W, W), BF),
        V((4, 8, 128), F32), V((8, 4, 8, 128), F32),
        V((C, 4, R, W), BF),
        [V((64, 16, 128), BF)] * C, V((C, 128, 16, 128), BF),
        V((C, 8, R, W), BF), V((C, 8, R, W), BF),
        V((8, 128, W), BF), V((C, 8, R, W), BF),
        V((8, 128), F32), V((8, 8, 128), F32),
        V((8, 128), F32), V((16, 8, 128), F32),
        V((C, 8, R, W), BF),
        [V((128, 16, 128), BF)] * C, V((C, 64, 16, 128), BF),
        V((C, 4, R, W), BF), V((4, 8, 128), F32), V((C, 4, R, W), BF),
        V((8, 128), jnp.int32), pltpu.SMEM((8, 128), jnp.int32),
        dma((16,)), dma((4,)), dma((16,)), dma((8,)), dma((8,)),
        dma((4,)), dma((4,)), dma((4,)), dma((4,)), dma((4,)), dma((4,)),
        dma((3,)), dma((8,)), dma((8,)), dma((16,)), dma((8,)), dma((1,)), dma((15,)),
    ]
    accum_new, update = pl.pallas_call(
        kernel,
        out_shape=(V((4, 128, W), F32), V((4, 8, 128, W), BF)),
        in_specs=[smem, smem] + [hbm] * 5,
        out_specs=(vmem, vmem),
        scratch_shapes=scratch,
        name="shampoo_step",
        compiler_params=pltpu.CompilerParams(
            collective_id=0, has_side_effects=True, vmem_limit_bytes=50 * 2**20
        ),
    )(
        block_owner,
        block_slot,
        local_grads.reshape(4, 4, 2, 128, W),
        left_root.reshape(8, 128, W),
        right_root.reshape(W, W),
        accumulator,
        momentum,
    )
    accum_new, update = pl.pallas_call(
        store,
        out_shape=(
            jax.ShapeDtypeStruct((4, 128, W), F32),
            jax.ShapeDtypeStruct((4, 8, 128, W), BF),
        ),
        in_specs=[vmem, vmem],
        out_specs=(hbm, hbm),
        scratch_shapes=[dma((8,))],
        name="store",
        compiler_params=pltpu.CompilerParams(vmem_limit_bytes=12 * 2**20),
    )(accum_new, update)
    return accum_new, update.reshape(4, W, W)


def solution(mesh):
    placed = (
        P("dp", "mp", None, None),
        P("mp", "dp", None, None),
        P("mp", "dp", None, None),
        P("mp", "dp", None),
        P("mp", "dp", None),
        P(),
        P(),
    )
    return jax.shard_map(
        shards,
        mesh=mesh,
        in_specs=placed,
        out_specs=(P("mp", "dp", None), P("mp", None, None)),
        check_vma=False,
    )
```

```python
import jax
import jax.numpy as jnp
from jax import lax
from jax.experimental import pallas as pl
from jax.experimental.pallas import tpu as pltpu
from jax.sharding import PartitionSpec as P

MESH = pl.DeviceIdType.MESH
BF = jnp.bfloat16
F32 = jnp.float32
beta_momentum = 0.9
eps_norm = 1e-06

CHUNKS = 4
ROWS = 32
W = 1024
COLUMN = ((0, 0), (0, 1), (1, 1), (3, 1), (1, 0), (3, 0), (2, 0), (2, 1))
NEAR, FAR = 0, 1
PLANE = (
    (2, 2), (1, 2), (2, 1), (3, 2), (2, 3), (0, 2), (2, 0), (1, 1),
    (3, 3), (1, 3), (3, 1), (0, 1), (1, 0), (0, 3), (3, 0),
)


def kernel(
    owner, slot, g, left, right, acc, mom, out_acc, out_upd,
    own, sib, t1p, t1m, t2p, t2m, accv, momv, lv, rv, ada, ar, sbuf, qb, p1, vb, gb, half, pp,
    nrm, nv, nt, nw, v2, wb, wp, hh, scl, up, invv, inv,
    s_own, s_in, s_sib, s_t1, s_t2, s_fa, s_fb, s_fc, s_ra, s_rb, s_rc, s_sm,
    s_a1, s_a2, s_sb, s_out, snd,
):
    dp = lax.axis_index("dp")
    mp = lax.axis_index("mp")
    y, c = dp // 2, dp % 2
    z, x = mp // 4, mp % 4
    piece_a, piece_h = mp // 8, mp % 8

    def col(dy, dc):
        return ((y + dy) % 4) * 2 + (c + dc) % 2

    def plane(dz, dx):
        return ((z + dz) % 4) * 4 + (x + dx) % 4

    def put(src, dst, ssem, rsem, device):
        pltpu.make_async_remote_copy(
            src_ref=src, dst_ref=dst, send_sem=snd.at[ssem], recv_sem=rsem,
            device_id=device, device_id_type=MESH,
        ).start()

    def keep(src, dst, sem):
        pltpu.make_async_copy(src, dst, sem).start()

    def await_bytes(ref, sem):
        pltpu.make_async_copy(ref, ref, sem).wait()

    seen_loads = set()

    def loaded(ref, n):
        if n not in seen_loads:
            seen_loads.add(n)
            await_bytes(ref, s_in.at[n])

    ends = []

    def place(b):
        return owner[b] * 8 + slot[b]

    def each_in_plane(body):
        for dz, dx in PLANE:
            body(plane(dz, dx))

    def piece(m):
        return pl.ds(pl.multiple_of((m // 8) * 16, 16), 16), pl.ds(
            pl.multiple_of((m % 8) * 128, 128), 128
        )

    up_dev = (col(1, 0), mp)
    down_dev = (col(3, 0), mp)
    sib_dev = (col(0, 1), mp)
    targets = ((y + 2) % 4, (y + 1) % 4, (y + 3) % 4, y)

    barrier = pltpu.get_barrier_semaphore()

    def greet(m):
        pl.semaphore_signal(barrier, inc=1, device_id=(dp, m), device_id_type=MESH)

    for dy, dc in COLUMN[1:]:
        pl.semaphore_signal(barrier, inc=1, device_id=(col(dy, dc), mp), device_id_type=MESH)
    each_in_plane(greet)
    for q in range(CHUNKS):
        for k in range(4):
            keep(
                g.at[:, targets[k], c, pl.ds(q * ROWS, ROWS), :],
                own.at[q, targets[k]],
                s_own.at[q * 4 + k],
            )
    lane = lax.broadcasted_iota(jnp.int32, (8, 128), 1)
    line = lax.broadcasted_iota(jnp.int32, (8, 128), 0)

    def fill(b, table):
        dy = (y + 4 - slot[b] // 2) % 4
        dc = (c + slot[b]) % 2
        across = jnp.where(dc == 1, 2 + dy // 2, 4 + dy // 2)
        seen = jnp.where(dy == 0, dc, jnp.where(dy == 2, 6 + dc, across))
        table = jnp.where((line == 0) & (lane == place(b)), b, table)
        return jnp.where((line == 1) & (lane == b), owner[b] * 8 + seen, table)

    invv[...] = lax.fori_loop(0, 64, fill, jnp.zeros((8, 128), jnp.int32))
    keep(invv, inv, s_in.at[4])
    keep(acc, accv, s_in.at[0])
    keep(right, rv, s_in.at[1])
    keep(left, lv, s_in.at[2])
    keep(mom, momv, s_in.at[3])

    pl.semaphore_wait(barrier, 22)

    def swap(q):
        for k in range(4):
            put(
                g.at[:, targets[k], 1 - c, pl.ds(q * ROWS, ROWS), :],
                sib.at[q, targets[k]],
                0,
                s_sib.at[q * 4 + k],
                sib_dev,
            )
            ends.append((sib.at[q, k], snd.at[0]))

    nrm[...] = jnp.zeros((8, 128), F32)
    for j in range(4):
        ada[j] = jnp.zeros((8, 128), F32)

    def both(q, k, j):
        t = targets[k]
        return own[q, t, j].astype(F32) + sib[q, t, j].astype(F32)

    def arrived(q, k):
        await_bytes(own.at[q, targets[k]], s_own.at[q * 4 + k])
        await_bytes(sib.at[q, targets[k]], s_sib.at[q * 4 + k])

    def fold(v):
        rows, lanes = v.shape
        v = jnp.sum(v.reshape(rows // 8, 8, lanes), axis=0)
        total = v[:, 0:128]
        for i in range(1, lanes // 128):
            total = total + v[:, i * 128 : (i + 1) * 128]
        return total

    def f0(q):
        if q + 1 < CHUNKS:
            swap(q + 1)
        arrived(q, 0)
        t = targets[0]
        for j in range(4):
            own[q, t, j] = both(q, 0, j).astype(BF)
        put(own.at[q, t, pl.ds(0, 2)], t1p.at[q], 1, s_t1.at[q * 2], up_dev)
        put(own.at[q, t, pl.ds(2, 2)], t1m.at[q], 1, s_t1.at[q * 2 + 1], down_dev)
        ends.extend([(t1p.at[q], snd.at[1]), (t1m.at[q], snd.at[1])])

    def f1(q):
        arrived(q, 1)
        arrived(q, 2)
        await_bytes(t1p.at[q], s_t1.at[q * 2])
        await_bytes(t1m.at[q], s_t1.at[q * 2 + 1])
        for j in range(4):
            value = both(q, 1, j)
            if j < 2:
                value = value + t1p[q, j].astype(F32)
            own[q, targets[1], j] = value.astype(BF)
        put(own.at[q, targets[1]], t2p.at[q], 2, s_t2.at[q * 2], up_dev)
        for j in range(4):
            value = both(q, 2, j)
            if j >= 2:
                value = value + t1m[q, j - 2].astype(F32)
            own[q, targets[2], j] = value.astype(BF)
        put(own.at[q, targets[2]], t2m.at[q], 2, s_t2.at[q * 2 + 1], down_dev)
        ends.extend([(t2p.at[q], snd.at[2]), (t2m.at[q], snd.at[2])])

    def f2(q):
        arrived(q, 3)
        await_bytes(t2p.at[q], s_t2.at[q * 2])
        await_bytes(t2m.at[q], s_t2.at[q * 2 + 1])
        loaded(accv, 0)
        rows = pl.ds(q * ROWS, ROWS)
        for j in range(4):
            total = both(q, 3, j) + t2p[q, j].astype(F32) + t2m[q, j].astype(F32)
            fresh = accv[j, rows, :] + total * total
            accv[j, rows, :] = fresh
            step = total * lax.rsqrt(fresh)
            ada[j] += fold(step * step)
            sbuf[q, j] = total.astype(BF)
        keep(accv.at[:, rows, :], out_acc.at[:, rows, :], s_out.at[q])

        def spread(m):
            r, l = piece(m)
            put(sbuf.at[q, :, r, l], qb[q].at[pl.ds(mp * 4, 4)], 3, s_fa.at[q], (dp, m))

        each_in_plane(spread)
        r, l = piece(mp)
        keep(sbuf.at[q, :, r, l], qb[q].at[pl.ds(mp * 4, 4)], s_fa.at[q])
        ends.extend([(qb[q].at[pl.ds(0, 60)], snd.at[3]), (out_acc.at[:, rows, :], s_out.at[q])])

    def share_adagrad():
        ar[dp] = ada[...]
        for dy, dc in COLUMN[1:]:
            put(ada, ar.at[dp], 4, s_sm.at[0], (col(dy, dc), mp))
        ends.append((ar.at[pl.ds(0, 7)], snd.at[4]))

    def f3(q):
        loaded(inv, 4)
        await_bytes(qb[q], s_fa.at[q])

        def pick(o, carry):
            for n in range(8):
                p1[q, o * 8 + n] = qb[q][inv[0, o * 8 + col(*COLUMN[n])]]
            return carry

        lax.fori_loop(0, 16, pick, 0)
        r, l = piece(mp)
        for part in (FAR, NEAR):
            sem = s_fb.at[q * 2 + part]

            def deal(o):
                put(
                    p1.at[q, pl.ds(o * 8 + part * 4, 4)],
                    vb.at[q, pl.ds(part * 4, 4), r, l],
                    5,
                    sem,
                    (dp, o),
                )

            each_in_plane(deal)
            keep(
                p1.at[q, pl.ds(mp * 8 + part * 4, 4)], vb.at[q, pl.ds(part * 4, 4), r, l], sem
            )
        ends.append((p1.at[q, pl.ds(0, 120)], snd.at[5]))

    def f4(q, part):
        await_bytes(vb.at[q, pl.ds(part * 4, 4)], s_fb.at[q * 2 + part])
        for k in range(part * 4, part * 4 + 4):
            if k:
                put(vb.at[q, k], gb.at[q, dp], 6, s_fc.at[q], (col(*COLUMN[k]), mp))
            else:
                keep(vb.at[q, k], gb.at[q, dp], s_fc.at[q])
        if part == FAR:
            ends.append((vb.at[q, pl.ds(0, 7)], snd.at[6]))

    def f5(q):
        loaded(rv, 1)
        await_bytes(gb.at[q], s_fc.at[q])

        def tile(n, carry):
            lanes = pl.ds(pl.multiple_of(n * 256, 256), 256)
            rows = gb[q].reshape(8 * ROWS, W)
            value = jnp.dot(rows, rv[:, lanes], preferred_element_type=F32)
            half[:, pl.ds(q * ROWS, ROWS), lanes] = value.astype(BF).reshape(8, ROWS, 256)
            return carry

        lax.fori_loop(0, 4, tile, 0)

    def product(q):
        loaded(lv, 2)

        def tile(n, carry):
            lanes = pl.ds(pl.multiple_of(n * 256, 256), 256)
            rows = lv[:, pl.ds(q * ROWS, ROWS), :].reshape(8 * ROWS, W)
            value = jnp.dot(rows, half[:, :, lanes].reshape(W, 256), preferred_element_type=F32)
            value = value.astype(BF)
            pp[q, :, :, lanes] = value.reshape(8, ROWS, 256)
            wide = value.astype(F32)
            nrm[...] += fold(wide * wide)
            return carry

        lax.fori_loop(0, 4, tile, 0)

    def r0(q):
        for k in range(8):
            d = col(*COLUMN[k])
            sem = s_ra.at[q * 2 + k // 4]
            if k:
                put(pp.at[q, d], v2.at[q, k], 7, sem, (d, mp))
            else:
                keep(pp.at[q, d], v2.at[q, k], sem)
        ends.append((pp.at[q, pl.ds(0, 7)], snd.at[7]))

    def share_norm():
        total = jnp.full((8, 128), jnp.sum(nrm[...]), F32)
        nrm[...] = total
        nv[dp] = total
        for dy, dc in COLUMN[1:]:
            put(nrm, nv.at[dp], 8, s_sm.at[1], (col(dy, dc), mp))
        ends.append((nv.at[pl.ds(0, 7)], snd.at[8]))

    def spread_norms():
        await_bytes(nv.at[pl.ds(0, 7)], s_sm.at[1])
        row = lax.broadcasted_iota(jnp.int32, (8, 128), 0)
        table = jnp.zeros((8, 128), F32)
        for s in range(8):
            table = jnp.where(row == s, nv[s], table)
        nt[...] = table
        nw[mp] = table

        def send(m):
            put(nt, nw.at[mp], 9, s_sm.at[2], (dp, m))

        each_in_plane(send)
        ends.append((nw.at[pl.ds(0, 15)], snd.at[9]))

    def r1(q, part):
        slots = pl.ds(part * 4, 4)
        await_bytes(v2.at[q, slots], s_ra.at[q * 2 + part])
        into = pl.ds(mp * 8 + part * 4, 4)

        def spread(m):
            r, l = piece(m)
            put(v2.at[q, slots, r, l], wb[q].at[into], 10, s_rb.at[q], (dp, m))

        each_in_plane(spread)
        r, l = piece(mp)
        keep(v2.at[q, slots, r, l], wb[q].at[into], s_rb.at[q])
        ends.append((wb[q].at[pl.ds(0, 60)], snd.at[10]))

    def r2(q):
        await_bytes(wb[q], s_rb.at[q])

        def pick(i, carry):
            for n in range(8):
                wp[q, i * 8 + n] = wb[q][inv[1, i * 8 + n]]
            return carry

        lax.fori_loop(0, 8, pick, 0)
        r, l = piece(mp)

        def deal(m):
            put(wp.at[q, pl.ds(m * 4, 4)], hh.at[q, :, r, l], 11, s_rc.at[q], (dp, m))

        each_in_plane(deal)
        keep(wp.at[q, pl.ds(mp * 4, 4)], hh.at[q, :, r, l], s_rc.at[q])
        ends.append((wp.at[q, pl.ds(0, 60)], snd.at[11]))

    def scales():
        await_bytes(ar.at[pl.ds(0, 7)], s_sm.at[0])
        await_bytes(nw.at[pl.ds(0, 15)], s_sm.at[2])
        loaded(momv, 3)
        row = lax.broadcasted_iota(jnp.int32, (8, 128), 0)
        for j in range(4):
            mine = nw[owner[mp * 4 + j]]
            pre = jnp.sum(jnp.where(row == slot[mp * 4 + j], mine, 0.0), axis=0, keepdims=True)
            ada_total = jnp.sum(ar[:, j])
            scl[j] = jnp.broadcast_to(jnp.sqrt(ada_total / (pre + eps_norm)), (8, 128))

    def rows_of(dy, q, first, count):
        return out_upd.at[pl.ds(first, count), col(dy, 0), pl.ds(q * ROWS, ROWS), :]

    def r3(q, first, count):
        if first == 0:
            await_bytes(hh.at[q], s_rc.at[q])
        for j in range(first, first + count):
            scale = jnp.concatenate([scl[j, 0:1, :]] * 8, axis=1)
            value = (
                beta_momentum * momv[j, pl.ds(q * ROWS, ROWS), :].astype(F32)
                + scale * hh[q, j].astype(F32)
            )
            up[q, j] = value.astype(BF)
        n = q * 2 + first // 2
        mine = up.at[q, pl.ds(first, count)]
        here = rows_of(0, q, first, count)
        put(mine, here, 12, s_a1.at[n * 2], up_dev)
        put(mine, here, 12, s_a1.at[n * 2 + 1], down_dev)
        put(mine, here, 14, s_sb.at[n * 4], sib_dev)
        keep(mine, here, s_out.at[4 + n])
        ends.extend([(here, snd.at[12]), (here, snd.at[12]), (here, snd.at[14])])
        ends.extend([(here, s_out.at[4 + n]), (here, s_sb.at[n * 4])])

    def r4(q, first, count):
        n = q * 2 + first // 2
        for k, dy in ((0, 3), (1, 1)):
            rows = rows_of(dy, q, first, count)
            await_bytes(rows, s_a1.at[n * 2 + k])
            part = rows_of(dy, q, first + k * (count // 2), count // 2)
            put(part, part, 13, s_a2.at[n * 2 + k], (up_dev, down_dev)[k])
            put(rows, rows, 14, s_sb.at[n * 4 + 1 + k], sib_dev)
            ends.extend([(part, snd.at[13]), (rows, snd.at[14]), (rows, s_sb.at[n * 4 + 1 + k])])

    def r5(q, first, count):
        n = q * 2 + first // 2
        for k in range(2):
            part = rows_of(2, q, first + k * (count // 2), count // 2)
            await_bytes(part, s_a2.at[n * 2 + k])
        rows = rows_of(2, q, first, count)
        put(rows, rows, 14, s_sb.at[n * 4 + 3], sib_dev)
        ends.extend([(rows, snd.at[14]), (rows, s_sb.at[n * 4 + 3])])

    swap(0)
    for stage, *which in (
        (f0, 0), (f0, 1), (f1, 0), (f1, 1), (f0, 2), (f0, 3), (f2, 0), (f2, 1), (f1, 2), (f3, 0),
        (f3, 1), (f1, 3), (f2, 2), (f4, 0, FAR), (f2, 3), (share_adagrad,), (f4, 0, NEAR),
        (f4, 1, FAR), (f4, 1, NEAR), (f3, 2), (f4, 2, FAR), (f3, 3), (f5, 1), (f4, 2, NEAR),
        (f4, 3, FAR), (f5, 0), (f4, 3, NEAR), (f5, 2), (f5, 3),
        (product, 0), (r0, 0), (product, 1), (product, 2), (product, 3), (share_norm,), (r0, 1),
        (r0, 2), (r1, 0, NEAR), (r0, 3), (r1, 0, FAR), (r1, 1, NEAR), (spread_norms,), (r2, 0),
        (r1, 1, FAR), (scales,), (r3, 0, 0, 4), (r1, 2, FAR), (r2, 1), (r1, 2, NEAR),
        (r1, 3, FAR), (r3, 1, 0, 4), (r4, 0, 0, 4), (r2, 2), (r1, 3, NEAR), (r4, 1, 0, 4),
        (r3, 2, 0, 4), (r2, 3), (r3, 3, 0, 2), (r3, 3, 2, 2), (r4, 2, 0, 4), (r4, 3, 0, 2),
        (r5, 0, 0, 4), (r4, 3, 2, 2), (r5, 2, 0, 4), (r5, 1, 0, 4), (r5, 3, 0, 2), (r5, 3, 2, 2),
    ):
        stage(*which)

    for ref, sem in ends:
        await_bytes(ref, sem)


def store(acc, upd, out_acc, out_upd, sems):
    copies = []
    for j in range(4):
        copies.append(pltpu.make_async_copy(acc.at[j], out_acc.at[j], sems.at[j]))
        copies.append(pltpu.make_async_copy(upd.at[j], out_upd.at[j], sems.at[4 + j]))
    for copy in copies:
        copy.start()
    for copy in copies:
        copy.wait()


def shards(local_grads, left_root, right_root, accumulator, momentum, block_owner, block_slot):
    hbm = pl.BlockSpec(memory_space=pl.ANY)
    vmem = pl.BlockSpec(memory_space=pltpu.VMEM)
    smem = pl.BlockSpec(memory_space=pltpu.SMEM)
    V = pltpu.VMEM
    dma = pltpu.SemaphoreType.DMA
    C, R = CHUNKS, ROWS
    scratch = [
        V((C, 4, 4, R, W), BF), V((C, 4, 4, R, W), BF),
        V((C, 2, R, W), BF), V((C, 2, R, W), BF),
        V((C, 4, R, W), BF), V((C, 4, R, W), BF),
        V((4, 128, W), F32), V((4, 128, W), BF),
        V((8, 128, W), BF), V((W, W), BF),
        V((4, 8, 128), F32), V((8, 4, 8, 128), F32),
        V((C, 4, R, W), BF),
        [V((64, 16, 128), BF)] * C, V((C, 128, 16, 128), BF),
        V((C, 8, R, W), BF), V((C, 8, R, W), BF),
        V((8, 128, W), BF), V((C, 8, R, W), BF),
        V((8, 128), F32), V((8, 8, 128), F32),
        V((8, 128), F32), V((16, 8, 128), F32),
        V((C, 8, R, W), BF),
        [V((128, 16, 128), BF)] * C, V((C, 64, 16, 128), BF),
        V((C, 4, R, W), BF), V((4, 8, 128), F32), V((C, 4, R, W), BF),
        V((8, 128), jnp.int32), pltpu.SMEM((8, 128), jnp.int32),
        dma((16,)), dma((5,)), dma((16,)), dma((8,)), dma((8,)),
        dma((4,)), dma((8,)), dma((4,)), dma((8,)), dma((4,)), dma((4,)),
        dma((3,)), dma((16,)), dma((16,)), dma((32,)), dma((12,)), dma((15,)),
    ]
    accum_new, update = pl.pallas_call(
        kernel,
        out_shape=(V((4, 128, W), F32), V((4, 8, 128, W), BF)),
        in_specs=[smem, smem] + [hbm] * 5,
        out_specs=(vmem, vmem),
        scratch_shapes=scratch,
        name="shampoo_step",
        compiler_params=pltpu.CompilerParams(
            collective_id=0, has_side_effects=True, vmem_limit_bytes=50 * 2**20
        ),
    )(
        block_owner,
        block_slot,
        local_grads.reshape(4, 4, 2, 128, W),
        left_root.reshape(8, 128, W),
        right_root.reshape(W, W),
        accumulator,
        momentum,
    )
    accum_new, update = pl.pallas_call(
        store,
        out_shape=(
            jax.ShapeDtypeStruct((4, 128, W), F32),
            jax.ShapeDtypeStruct((4, 8, 128, W), BF),
        ),
        in_specs=[vmem, vmem],
        out_specs=(hbm, hbm),
        scratch_shapes=[dma((8,))],
        name="store",
        compiler_params=pltpu.CompilerParams(vmem_limit_bytes=12 * 2**20),
    )(accum_new, update)
    return accum_new, update.reshape(4, W, W)


def solution(mesh):
    placed = (
        P("dp", "mp", None, None),
        P("mp", "dp", None, None),
        P("mp", "dp", None, None),
        P("mp", "dp", None),
        P("mp", "dp", None),
        P(),
        P(),
    )
    return jax.shard_map(
        shards,
        mesh=mesh,
        in_specs=placed,
        out_specs=(P("mp", "dp", None), P("mp", None, None)),
        check_vma=False,
    )
```

```python
import jax
import jax.numpy as jnp
from jax import lax
from jax.experimental import pallas as pl
from jax.experimental.pallas import tpu as pltpu
from jax.sharding import PartitionSpec as P

MESH = pl.DeviceIdType.MESH
BF = jnp.bfloat16
F32 = jnp.float32
beta_momentum = 0.9
eps_norm = 1e-06

CHUNKS = 4
TILE = 512
ROWS = 32
W = 1024
COLUMN = ((0, 0), (0, 1), (1, 1), (3, 1), (1, 0), (3, 0), (2, 0), (2, 1))
NEAR, FAR = 0, 1
PLANE = (
    (2, 2), (1, 2), (2, 1), (3, 2), (2, 3), (0, 2), (2, 0), (1, 1),
    (3, 3), (1, 3), (3, 1), (0, 1), (1, 0), (0, 3), (3, 0),
)


def kernel(
    owner, slot, g, left, right, acc, mom, out_acc, out_upd,
    own, sib, t1p, t1m, t2p, t2m, accv, momv, lv, rv, ada, adt, ar, sbuf, qb, p1, vb, gb, half, pp,
    nrm, nv, nt, nw, v2, wb, wp, hh, scl, up, invv, inv,
    s_own, s_in, s_sib, s_t1, s_t2, s_fa, s_fb, s_fc, s_ra, s_rb, s_rc, s_sm,
    s_a1, s_a2, s_sb, s_out, snd,
):
    dp = lax.axis_index("dp")
    mp = lax.axis_index("mp")
    y, c = dp // 2, dp % 2
    z, x = mp // 4, mp % 4
    piece_a, piece_h = mp // 8, mp % 8

    def col(dy, dc):
        return ((y + dy) % 4) * 2 + (c + dc) % 2

    def plane(dz, dx):
        return ((z + dz) % 4) * 4 + (x + dx) % 4

    def put(src, dst, ssem, rsem, device):
        pltpu.make_async_remote_copy(
            src_ref=src, dst_ref=dst, send_sem=snd.at[ssem], recv_sem=rsem,
            device_id=device, device_id_type=MESH,
        ).start()

    def keep(src, dst, sem):
        pltpu.make_async_copy(src, dst, sem).start()

    def await_bytes(ref, sem):
        pltpu.make_async_copy(ref, ref, sem).wait()

    seen_loads = set()

    def loaded(ref, n):
        if n not in seen_loads:
            seen_loads.add(n)
            await_bytes(ref, s_in.at[n])

    ends = []

    def place(b):
        return owner[b] * 8 + slot[b]

    def each_in_plane(body):
        for dz, dx in PLANE:
            body(plane(dz, dx))

    def piece(m):
        return pl.ds(pl.multiple_of((m // 8) * 16, 16), 16), pl.ds(
            pl.multiple_of((m % 8) * 128, 128), 128
        )

    up_dev = (col(1, 0), mp)
    down_dev = (col(3, 0), mp)
    sib_dev = (col(0, 1), mp)
    targets = ((y + 2) % 4, (y + 1) % 4, (y + 3) % 4, y)

    barrier = pltpu.get_barrier_semaphore()

    def greet(m):
        pl.semaphore_signal(barrier, inc=1, device_id=(dp, m), device_id_type=MESH)

    for dy, dc in COLUMN[1:]:
        pl.semaphore_signal(barrier, inc=1, device_id=(col(dy, dc), mp), device_id_type=MESH)
    each_in_plane(greet)
    for q in range(CHUNKS):
        for k in range(4):
            keep(
                g.at[:, targets[k], c, pl.ds(q * ROWS, ROWS), :],
                own.at[q, targets[k]],
                s_own.at[q * 4 + k],
            )
    lane = lax.broadcasted_iota(jnp.int32, (8, 128), 1)
    line = lax.broadcasted_iota(jnp.int32, (8, 128), 0)

    def fill(b, table):
        dy = (y + 4 - slot[b] // 2) % 4
        dc = (c + slot[b]) % 2
        across = jnp.where(dc == 1, 2 + dy // 2, 4 + dy // 2)
        seen = jnp.where(dy == 0, dc, jnp.where(dy == 2, 6 + dc, across))
        table = jnp.where((line == 0) & (lane == place(b)), b, table)
        return jnp.where((line == 1) & (lane == b), owner[b] * 8 + seen, table)

    invv[...] = lax.fori_loop(0, 64, fill, jnp.zeros((8, 128), jnp.int32))
    keep(invv, inv, s_in.at[4])
    keep(acc, accv, s_in.at[0])
    keep(right, rv, s_in.at[1])
    keep(left, lv, s_in.at[2])
    keep(mom, momv, s_in.at[3])

    pl.semaphore_wait(barrier, 22)

    def swap(q):
        for k in range(4):
            put(
                g.at[:, targets[k], 1 - c, pl.ds(q * ROWS, ROWS), :],
                sib.at[q, targets[k]],
                0,
                s_sib.at[q * 4 + k],
                sib_dev,
            )
            ends.append((sib.at[q, k], snd.at[0]))

    nrm[...] = jnp.zeros((8, 128), F32)
    for j in range(4):
        ada[j] = jnp.zeros((8, 128), F32)

    def both(q, k, j):
        t = targets[k]
        return own[q, t, j].astype(F32) + sib[q, t, j].astype(F32)

    def arrived(q, k):
        await_bytes(own.at[q, targets[k]], s_own.at[q * 4 + k])
        await_bytes(sib.at[q, targets[k]], s_sib.at[q * 4 + k])

    def fold(v):
        rows, lanes = v.shape
        v = jnp.sum(v.reshape(rows // 8, 8, lanes), axis=0)
        total = v[:, 0:128]
        for i in range(1, lanes // 128):
            total = total + v[:, i * 128 : (i + 1) * 128]
        return total

    def f0(q):
        if q + 1 < CHUNKS:
            swap(q + 1)
        arrived(q, 0)
        t = targets[0]
        for j in range(4):
            own[q, t, j] = both(q, 0, j).astype(BF)
        put(own.at[q, t, pl.ds(0, 2)], t1p.at[q], 1, s_t1.at[q * 2], up_dev)
        put(own.at[q, t, pl.ds(2, 2)], t1m.at[q], 1, s_t1.at[q * 2 + 1], down_dev)
        ends.extend([(t1p.at[q], snd.at[1]), (t1m.at[q], snd.at[1])])

    def f1(q):
        arrived(q, 1)
        arrived(q, 2)
        await_bytes(t1p.at[q], s_t1.at[q * 2])
        await_bytes(t1m.at[q], s_t1.at[q * 2 + 1])
        for j in range(4):
            value = both(q, 1, j)
            if j < 2:
                value = value + t1p[q, j].astype(F32)
            own[q, targets[1], j] = value.astype(BF)
        put(own.at[q, targets[1]], t2p.at[q], 2, s_t2.at[q * 2], up_dev)
        for j in range(4):
            value = both(q, 2, j)
            if j >= 2:
                value = value + t1m[q, j - 2].astype(F32)
            own[q, targets[2], j] = value.astype(BF)
        put(own.at[q, targets[2]], t2m.at[q], 2, s_t2.at[q * 2 + 1], down_dev)
        ends.extend([(t2p.at[q], snd.at[2]), (t2m.at[q], snd.at[2])])

    def f2(q):
        arrived(q, 3)
        await_bytes(t2p.at[q], s_t2.at[q * 2])
        await_bytes(t2m.at[q], s_t2.at[q * 2 + 1])
        loaded(accv, 0)
        rows = pl.ds(q * ROWS, ROWS)
        for j in range(4):
            total = both(q, 3, j) + t2p[q, j].astype(F32) + t2m[q, j].astype(F32)
            fresh = accv[j, rows, :] + total * total
            accv[j, rows, :] = fresh
            step = total * lax.rsqrt(fresh)
            ada[j] += fold(step * step)
            sbuf[q, j] = total.astype(BF)
        keep(accv.at[:, rows, :], out_acc.at[:, rows, :], s_out.at[q])

        def spread(m):
            r, l = piece(m)
            put(sbuf.at[q, :, r, l], qb[q].at[pl.ds(mp * 4, 4)], 3, s_fa.at[q], (dp, m))

        each_in_plane(spread)
        r, l = piece(mp)
        keep(sbuf.at[q, :, r, l], qb[q].at[pl.ds(mp * 4, 4)], s_fa.at[q])
        ends.extend([(qb[q].at[pl.ds(0, 60)], snd.at[3]), (out_acc.at[:, rows, :], s_out.at[q])])

    def share_adagrad():
        row = lax.broadcasted_iota(jnp.int32, (8, 128), 0)
        table = jnp.zeros((8, 128), F32)
        for j in range(4):
            table = jnp.where(row == j, jnp.sum(ada[j]), table)
        adt[...] = table
        ar[dp] = table
        for dy, dc in COLUMN[1:]:
            put(adt, ar.at[dp], 4, s_sm.at[0], (col(dy, dc), mp))
        ends.append((ar.at[pl.ds(0, 7)], snd.at[4]))

    def f3(q):
        loaded(inv, 4)
        await_bytes(qb[q], s_fa.at[q])

        def pick(o, carry):
            for n in range(8):
                p1[q, o * 8 + n] = qb[q][inv[0, o * 8 + col(*COLUMN[n])]]
            return carry

        lax.fori_loop(0, 16, pick, 0)
        r, l = piece(mp)
        for part in (FAR, NEAR):
            sem = s_fb.at[q * 2 + part]

            def deal(o):
                put(
                    p1.at[q, pl.ds(o * 8 + part * 4, 4)],
                    vb.at[q, pl.ds(part * 4, 4), r, l],
                    5,
                    sem,
                    (dp, o),
                )

            each_in_plane(deal)
            keep(
                p1.at[q, pl.ds(mp * 8 + part * 4, 4)], vb.at[q, pl.ds(part * 4, 4), r, l], sem
            )
        ends.append((p1.at[q, pl.ds(0, 120)], snd.at[5]))

    def f4(q, part):
        await_bytes(vb.at[q, pl.ds(part * 4, 4)], s_fb.at[q * 2 + part])
        for k in range(part * 4, part * 4 + 4):
            if k:
                put(vb.at[q, k], gb.at[q, dp], 6, s_fc.at[q], (col(*COLUMN[k]), mp))
            else:
                keep(vb.at[q, k], gb.at[q, dp], s_fc.at[q])
        if part == FAR:
            ends.append((vb.at[q, pl.ds(0, 7)], snd.at[6]))

    def half_tile(q, lanes):
        rows = gb[q].reshape(8 * ROWS, W)
        value = jnp.dot(rows, rv[:, lanes], preferred_element_type=F32)
        half[:, pl.ds(q * ROWS, ROWS), lanes] = value.astype(BF).reshape(8, ROWS, TILE)

    def product_tile(q, lanes):
        rows = lv[:, pl.ds(q * ROWS, ROWS), :].reshape(8 * ROWS, W)
        value = jnp.dot(rows, half[:, :, lanes].reshape(W, TILE), preferred_element_type=F32)
        value = value.astype(BF)
        pp[q, :, :, lanes] = value.reshape(8, ROWS, TILE)
        wide = value.astype(F32)
        nrm[...] += fold(wide * wide)

    def by_tiles(body, q):
        def step(n, carry):
            body(q, pl.ds(pl.multiple_of(n * TILE, TILE), TILE))
            return carry

        lax.fori_loop(0, W // TILE, step, 0)

    def f5(q):
        loaded(rv, 1)
        await_bytes(gb.at[q], s_fc.at[q])
        by_tiles(half_tile, q)

    def product(q):
        by_tiles(product_tile, q)

    def give(q, ks, lanes):
        for k in ks:
            d = col(*COLUMN[k])
            sem = s_ra.at[q * 2 + k // 4]
            if k:
                put(pp.at[q, d, :, lanes], v2.at[q, k, :, lanes], 7, sem, (d, mp))
            else:
                keep(pp.at[q, d, :, lanes], v2.at[q, k, :, lanes], sem)

    def r0(q):
        give(q, range(8), pl.ds(0, W))
        ends.append((pp.at[q, pl.ds(0, 7)], snd.at[7]))

    def turn(q):
        loaded(lv, 2)
        await_bytes(gb.at[q], s_fc.at[q])
        first, second = pl.ds(0, TILE), pl.ds(TILE, TILE)
        half_tile(q, first)
        product_tile(0, first)
        give(0, range(6), first)
        half_tile(q, second)
        product_tile(0, second)
        give(0, range(4), second)
        give(0, (6, 7), first)
        give(0, range(4, 8), second)
        ends.append((pp.at[0, pl.ds(0, 7)], snd.at[7]))

    line0 = pl.ds(0, 1)

    def share_norm():
        total = jnp.full((1, 128), jnp.sum(nrm[...]), F32)
        nrm[0:1, :] = total
        nv[dp, 0:1, :] = total
        for dy, dc in COLUMN[1:]:
            put(nrm.at[line0], nv.at[dp, line0], 8, s_sm.at[1], (col(dy, dc), mp))
        ends.append((nv.at[pl.ds(0, 7), line0], snd.at[8]))

    def spread_norms():
        await_bytes(nv.at[pl.ds(0, 7), line0], s_sm.at[1])
        at = lax.broadcasted_iota(jnp.int32, (1, 128), 1)
        table = jnp.zeros((1, 128), F32)
        for s in range(8):
            table = jnp.where(at == s, nv[s, 0:1, :], table)
        nt[0:1, :] = table
        nw[mp, 0:1, :] = table

        def send(m):
            put(nt.at[line0], nw.at[mp, line0], 9, s_sm.at[2], (dp, m))

        each_in_plane(send)
        ends.append((nw.at[pl.ds(0, 15), line0], snd.at[9]))

    def r1(q, part):
        slots = pl.ds(part * 4, 4)
        await_bytes(v2.at[q, slots], s_ra.at[q * 2 + part])
        into = pl.ds(mp * 8 + part * 4, 4)

        def spread(m):
            r, l = piece(m)
            put(v2.at[q, slots, r, l], wb[q].at[into], 10, s_rb.at[q], (dp, m))

        each_in_plane(spread)
        r, l = piece(mp)
        keep(v2.at[q, slots, r, l], wb[q].at[into], s_rb.at[q])
        ends.append((wb[q].at[pl.ds(0, 60)], snd.at[10]))

    def r2(q):
        await_bytes(wb[q], s_rb.at[q])

        def pick(i, carry):
            for n in range(8):
                wp[q, i * 8 + n] = wb[q][inv[1, i * 8 + n]]
            return carry

        lax.fori_loop(0, 8, pick, 0)
        r, l = piece(mp)

        def deal(m):
            put(wp.at[q, pl.ds(m * 4, 4)], hh.at[q, :, r, l], 11, s_rc.at[q], (dp, m))

        each_in_plane(deal)
        keep(wp.at[q, pl.ds(mp * 4, 4)], hh.at[q, :, r, l], s_rc.at[q])
        ends.append((wp.at[q, pl.ds(0, 60)], snd.at[11]))

    def scales():
        await_bytes(ar.at[pl.ds(0, 7)], s_sm.at[0])
        await_bytes(nw.at[pl.ds(0, 15), line0], s_sm.at[2])
        loaded(momv, 3)
        at = lax.broadcasted_iota(jnp.int32, (1, 128), 1)
        sums = jnp.sum(ar[...], axis=0)
        for j in range(4):
            mine = nw[owner[mp * 4 + j], 0:1, :]
            pre = jnp.sum(jnp.where(at == slot[mp * 4 + j], mine, 0.0), axis=1, keepdims=True)
            scale = jnp.sqrt(sums[j : j + 1, :] / (pre + eps_norm))
            scl[j] = jnp.broadcast_to(scale, (8, 128))

    def rows_of(dy, q, first, count):
        return out_upd.at[pl.ds(first, count), col(dy, 0), pl.ds(q * ROWS, ROWS), :]

    def r3(q, first, count):
        if first == 0:
            await_bytes(hh.at[q], s_rc.at[q])
        for j in range(first, first + count):
            scale = jnp.concatenate([scl[j, 0:1, :]] * 8, axis=1)
            value = (
                beta_momentum * momv[j, pl.ds(q * ROWS, ROWS), :].astype(F32)
                + scale * hh[q, j].astype(F32)
            )
            up[q, j] = value.astype(BF)
        n = q * 2 + first // 2
        mine = up.at[q, pl.ds(first, count)]
        here = rows_of(0, q, first, count)
        put(mine, here, 12, s_a1.at[n * 2], up_dev)
        put(mine, here, 12, s_a1.at[n * 2 + 1], down_dev)
        put(mine, here, 14, s_sb.at[n * 4], sib_dev)
        keep(mine, here, s_out.at[4 + n])
        ends.extend([(here, snd.at[12]), (here, snd.at[12]), (here, snd.at[14])])
        ends.extend([(here, s_out.at[4 + n]), (here, s_sb.at[n * 4])])

    def r4(q, first, count):
        n = q * 2 + first // 2
        for k, dy in ((0, 3), (1, 1)):
            rows = rows_of(dy, q, first, count)
            await_bytes(rows, s_a1.at[n * 2 + k])
            part = rows_of(dy, q, first + k * (count // 2), count // 2)
            put(part, part, 13, s_a2.at[n * 2 + k], (up_dev, down_dev)[k])
            put(rows, rows, 14, s_sb.at[n * 4 + 1 + k], sib_dev)
            ends.extend([(part, snd.at[13]), (rows, snd.at[14]), (rows, s_sb.at[n * 4 + 1 + k])])

    def r5(q, first, count):
        n = q * 2 + first // 2
        for k in range(2):
            part = rows_of(2, q, first + k * (count // 2), count // 2)
            await_bytes(part, s_a2.at[n * 2 + k])
        rows = rows_of(2, q, first, count)
        put(rows, rows, 14, s_sb.at[n * 4 + 3], sib_dev)
        ends.extend([(rows, snd.at[14]), (rows, s_sb.at[n * 4 + 3])])

    swap(0)
    for stage, *which in (
        (f0, 0), (f0, 1), (f1, 0), (f1, 1), (f0, 2), (f0, 3), (f2, 0), (f2, 1), (f1, 2), (f3, 0),
        (f3, 1), (f1, 3), (f2, 2), (f4, 0, FAR), (f2, 3), (f4, 0, NEAR),
        (f4, 1, FAR), (f4, 1, NEAR), (f3, 2), (f4, 2, FAR), (f3, 3), (f5, 1), (f4, 2, NEAR),
        (f4, 3, FAR), (f5, 0), (f4, 3, NEAR), (share_adagrad,), (f5, 2),
        (turn, 3),
        (product, 1), (product, 2), (product, 3), (share_norm,), (r0, 1),
        (r0, 2), (r1, 0, NEAR), (r0, 3), (r1, 0, FAR), (r1, 1, NEAR), (spread_norms,), (r2, 0),
        (r1, 1, FAR), (scales,), (r3, 0, 0, 4), (r1, 2, FAR), (r2, 1), (r1, 2, NEAR),
        (r1, 3, FAR), (r3, 1, 0, 4), (r4, 0, 0, 4), (r2, 2), (r1, 3, NEAR), (r4, 1, 0, 4),
        (r3, 2, 0, 4), (r2, 3), (r3, 3, 0, 2), (r3, 3, 2, 2), (r4, 2, 0, 4), (r4, 3, 0, 2),
        (r5, 0, 0, 4), (r4, 3, 2, 2), (r5, 2, 0, 4), (r5, 1, 0, 4), (r5, 3, 0, 2), (r5, 3, 2, 2),
    ):
        stage(*which)

    for ref, sem in ends:
        await_bytes(ref, sem)


def store(acc, upd, out_acc, out_upd, sems):
    copies = []
    for j in range(4):
        copies.append(pltpu.make_async_copy(acc.at[j], out_acc.at[j], sems.at[j]))
        copies.append(pltpu.make_async_copy(upd.at[j], out_upd.at[j], sems.at[4 + j]))
    for copy in copies:
        copy.start()
    for copy in copies:
        copy.wait()


def shards(local_grads, left_root, right_root, accumulator, momentum, block_owner, block_slot):
    hbm = pl.BlockSpec(memory_space=pl.ANY)
    vmem = pl.BlockSpec(memory_space=pltpu.VMEM)
    smem = pl.BlockSpec(memory_space=pltpu.SMEM)
    V = pltpu.VMEM
    dma = pltpu.SemaphoreType.DMA
    C, R = CHUNKS, ROWS
    scratch = [
        V((C, 4, 4, R, W), BF), V((C, 4, 4, R, W), BF),
        V((C, 2, R, W), BF), V((C, 2, R, W), BF),
        V((C, 4, R, W), BF), V((C, 4, R, W), BF),
        V((4, 128, W), F32), V((4, 128, W), BF),
        V((8, 128, W), BF), V((W, W), BF),
        V((4, 8, 128), F32), V((8, 128), F32), V((8, 8, 128), F32),
        V((C, 4, R, W), BF),
        [V((64, 16, 128), BF)] * C, V((C, 128, 16, 128), BF),
        V((C, 8, R, W), BF), V((C, 8, R, W), BF),
        V((8, 128, W), BF), V((C, 8, R, W), BF),
        V((8, 128), F32), V((8, 8, 128), F32),
        V((8, 128), F32), V((16, 8, 128), F32),
        V((C, 8, R, W), BF),
        [V((128, 16, 128), BF)] * C, V((C, 64, 16, 128), BF),
        V((C, 4, R, W), BF), V((4, 8, 128), F32), V((C, 4, R, W), BF),
        V((8, 128), jnp.int32), pltpu.SMEM((8, 128), jnp.int32),
        dma((16,)), dma((5,)), dma((16,)), dma((8,)), dma((8,)),
        dma((4,)), dma((8,)), dma((4,)), dma((8,)), dma((4,)), dma((4,)),
        dma((3,)), dma((16,)), dma((16,)), dma((32,)), dma((12,)), dma((15,)),
    ]
    accum_new, update = pl.pallas_call(
        kernel,
        out_shape=(V((4, 128, W), F32), V((4, 8, 128, W), BF)),
        in_specs=[smem, smem] + [hbm] * 5,
        out_specs=(vmem, vmem),
        scratch_shapes=scratch,
        name="shampoo_step",
        compiler_params=pltpu.CompilerParams(
            collective_id=0, has_side_effects=True, vmem_limit_bytes=50 * 2**20
        ),
    )(
        block_owner,
        block_slot,
        local_grads.reshape(4, 4, 2, 128, W),
        left_root.reshape(8, 128, W),
        right_root.reshape(W, W),
        accumulator,
        momentum,
    )
    accum_new, update = pl.pallas_call(
        store,
        out_shape=(
            jax.ShapeDtypeStruct((4, 128, W), F32),
            jax.ShapeDtypeStruct((4, 8, 128, W), BF),
        ),
        in_specs=[vmem, vmem],
        out_specs=(hbm, hbm),
        scratch_shapes=[dma((8,))],
        name="store",
        compiler_params=pltpu.CompilerParams(vmem_limit_bytes=12 * 2**20),
    )(accum_new, update)
    return accum_new, update.reshape(4, W, W)


def solution(mesh):
    placed = (
        P("dp", "mp", None, None),
        P("mp", "dp", None, None),
        P("mp", "dp", None, None),
        P("mp", "dp", None),
        P("mp", "dp", None),
        P(),
        P(),
    )
    return jax.shard_map(
        shards,
        mesh=mesh,
        in_specs=placed,
        out_specs=(P("mp", "dp", None), P("mp", None, None)),
        check_vma=False,
    )
```

```python
import jax
import jax.numpy as jnp
from jax import lax
from jax.experimental import pallas as pl
from jax.experimental.pallas import tpu as pltpu
from jax.sharding import PartitionSpec as P

MESH = pl.DeviceIdType.MESH
BF = jnp.bfloat16
F32 = jnp.float32
beta_momentum = 0.9
eps_norm = 1e-06

CHUNKS = 4
TILE = 512
ROWS = 32
W = 1024
COLUMN = ((0, 0), (0, 1), (1, 1), (3, 1), (1, 0), (3, 0), (2, 0), (2, 1))
NEAR, FAR = 0, 1
PLANE = (
    (2, 2), (1, 2), (2, 1), (3, 2), (2, 3), (0, 2), (2, 0), (1, 1),
    (3, 3), (1, 3), (3, 1), (0, 1), (1, 0), (0, 3), (3, 0),
)


def kernel(
    owner, slot, g, left, right, acc, mom, out_acc, out_upd,
    own, sib, t1p, t1m, t2p, t2m, accv, momv, lv, rv, ada, adt, ar, sbuf, qb, p1, vb, gb, half, pp,
    nrm, nv, nt, nw, v2, wb, wp, hh, scl, up, invv, inv,
    s_own, s_in, s_sib, s_t1, s_t2, s_fa, s_fb, s_fc, s_ra, s_rb, s_rc, s_sm,
    s_a1, s_a2, s_sb, s_out, snd,
):
    dp = lax.axis_index("dp")
    mp = lax.axis_index("mp")
    y, c = dp // 2, dp % 2
    z, x = mp // 4, mp % 4
    piece_a, piece_h = mp // 8, mp % 8

    def col(dy, dc):
        return ((y + dy) % 4) * 2 + (c + dc) % 2

    def plane(dz, dx):
        return ((z + dz + c * (4 + dx - dz)) % 4) * 4 + (x + dx + c * (4 + dz - dx)) % 4

    def put(src, dst, ssem, rsem, device):
        pltpu.make_async_remote_copy(
            src_ref=src, dst_ref=dst, send_sem=snd.at[ssem], recv_sem=rsem,
            device_id=device, device_id_type=MESH,
        ).start()

    def keep(src, dst, sem):
        pltpu.make_async_copy(src, dst, sem).start()

    def await_bytes(ref, sem):
        pltpu.make_async_copy(ref, ref, sem).wait()

    seen_loads = set()

    def loaded(ref, n):
        if n not in seen_loads:
            seen_loads.add(n)
            await_bytes(ref, s_in.at[n])

    ends = []

    def place(b):
        return owner[b] * 8 + slot[b]

    def each_in_plane(body):
        for dz, dx in PLANE:
            body(plane(dz, dx))

    def piece(m):
        return pl.ds(pl.multiple_of((m // 8) * 16, 16), 16), pl.ds(
            pl.multiple_of((m % 8) * 128, 128), 128
        )

    up_dev = (col(1, 0), mp)
    down_dev = (col(3, 0), mp)
    sib_dev = (col(0, 1), mp)
    targets = ((y + 2) % 4, (y + 1) % 4, (y + 3) % 4, y)

    barrier = pltpu.get_barrier_semaphore()

    def greet(m):
        pl.semaphore_signal(barrier, inc=1, device_id=(dp, m), device_id_type=MESH)

    for dy, dc in COLUMN[1:]:
        pl.semaphore_signal(barrier, inc=1, device_id=(col(dy, dc), mp), device_id_type=MESH)
    each_in_plane(greet)
    for q in range(CHUNKS):
        for k in range(4):
            keep(
                g.at[:, targets[k], c, pl.ds(q * ROWS, ROWS), :],
                own.at[q, targets[k]],
                s_own.at[q * 4 + k],
            )
    lane = lax.broadcasted_iota(jnp.int32, (8, 128), 1)
    line = lax.broadcasted_iota(jnp.int32, (8, 128), 0)

    def fill(b, table):
        dy = (y + 4 - slot[b] // 2) % 4
        dc = (c + slot[b]) % 2
        across = jnp.where(dc == 1, 2 + dy // 2, 4 + dy // 2)
        seen = jnp.where(dy == 0, dc, jnp.where(dy == 2, 6 + dc, across))
        table = jnp.where((line == 0) & (lane == place(b)), b, table)
        return jnp.where((line == 1) & (lane == b), owner[b] * 8 + seen, table)

    invv[...] = lax.fori_loop(0, 64, fill, jnp.zeros((8, 128), jnp.int32))
    keep(invv, inv, s_in.at[4])
    keep(acc, accv, s_in.at[0])
    keep(right, rv, s_in.at[1])
    keep(left, lv, s_in.at[2])
    keep(mom, momv, s_in.at[3])

    pl.semaphore_wait(barrier, 22)

    def swap(q):
        for k in range(4):
            put(
                g.at[:, targets[k], 1 - c, pl.ds(q * ROWS, ROWS), :],
                sib.at[q, targets[k]],
                0,
                s_sib.at[q * 4 + k],
                sib_dev,
            )
            ends.append((sib.at[q, k], snd.at[0]))

    nrm[...] = jnp.zeros((8, 128), F32)
    for j in range(4):
        ada[j] = jnp.zeros((8, 128), F32)

    def both(q, k, j):
        t = targets[k]
        return own[q, t, j].astype(F32) + sib[q, t, j].astype(F32)

    def arrived(q, k):
        await_bytes(own.at[q, targets[k]], s_own.at[q * 4 + k])
        await_bytes(sib.at[q, targets[k]], s_sib.at[q * 4 + k])

    def fold(v):
        rows, lanes = v.shape
        v = jnp.sum(v.reshape(rows // 8, 8, lanes), axis=0)
        total = v[:, 0:128]
        for i in range(1, lanes // 128):
            total = total + v[:, i * 128 : (i + 1) * 128]
        return total

    def f0(q):
        if q + 1 < CHUNKS:
            swap(q + 1)
        arrived(q, 0)
        t = targets[0]
        for j in range(4):
            own[q, t, j] = both(q, 0, j).astype(BF)
        put(own.at[q, t, pl.ds(0, 2)], t1p.at[q], 1, s_t1.at[q * 2], up_dev)
        put(own.at[q, t, pl.ds(2, 2)], t1m.at[q], 1, s_t1.at[q * 2 + 1], down_dev)
        ends.extend([(t1p.at[q], snd.at[1]), (t1m.at[q], snd.at[1])])

    def f1(q):
        arrived(q, 1)
        arrived(q, 2)
        await_bytes(t1p.at[q], s_t1.at[q * 2])
        await_bytes(t1m.at[q], s_t1.at[q * 2 + 1])
        for j in range(4):
            value = both(q, 1, j)
            if j < 2:
                value = value + t1p[q, j].astype(F32)
            own[q, targets[1], j] = value.astype(BF)
        put(own.at[q, targets[1]], t2p.at[q], 2, s_t2.at[q * 2], up_dev)
        for j in range(4):
            value = both(q, 2, j)
            if j >= 2:
                value = value + t1m[q, j - 2].astype(F32)
            own[q, targets[2], j] = value.astype(BF)
        put(own.at[q, targets[2]], t2m.at[q], 2, s_t2.at[q * 2 + 1], down_dev)
        ends.extend([(t2p.at[q], snd.at[2]), (t2m.at[q], snd.at[2])])

    def f2(q):
        arrived(q, 3)
        await_bytes(t2p.at[q], s_t2.at[q * 2])
        await_bytes(t2m.at[q], s_t2.at[q * 2 + 1])
        loaded(accv, 0)
        rows = pl.ds(q * ROWS, ROWS)
        for j in range(4):
            total = both(q, 3, j) + t2p[q, j].astype(F32) + t2m[q, j].astype(F32)
            fresh = accv[j, rows, :] + total * total
            accv[j, rows, :] = fresh
            step = total * lax.rsqrt(fresh)
            ada[j] += fold(step * step)
            sbuf[q, j] = total.astype(BF)
        keep(accv.at[:, rows, :], out_acc.at[:, rows, :], s_out.at[q])

        def spread(m):
            r, l = piece(m)
            put(sbuf.at[q, :, r, l], qb[q].at[pl.ds(mp * 4, 4)], 3, s_fa.at[q], (dp, m))

        each_in_plane(spread)
        r, l = piece(mp)
        keep(sbuf.at[q, :, r, l], qb[q].at[pl.ds(mp * 4, 4)], s_fa.at[q])
        ends.extend([(qb[q].at[pl.ds(0, 60)], snd.at[3]), (out_acc.at[:, rows, :], s_out.at[q])])

    def share_adagrad():
        row = lax.broadcasted_iota(jnp.int32, (8, 128), 0)
        table = jnp.zeros((8, 128), F32)
        for j in range(4):
            table = jnp.where(row == j, jnp.sum(ada[j]), table)
        adt[...] = table
        ar[dp] = table
        for dy, dc in COLUMN[1:]:
            put(adt, ar.at[dp], 4, s_sm.at[0], (col(dy, dc), mp))
        ends.append((ar.at[pl.ds(0, 7)], snd.at[4]))

    def f3(q):
        loaded(inv, 4)
        await_bytes(qb[q], s_fa.at[q])

        def pick(o, carry):
            for n in range(8):
                p1[q, o * 8 + n] = qb[q][inv[0, o * 8 + col(*COLUMN[n])]]
            return carry

        lax.fori_loop(0, 16, pick, 0)
        r, l = piece(mp)
        for part in (FAR, NEAR):
            sem = s_fb.at[q * 2 + part]

            def deal(o):
                put(
                    p1.at[q, pl.ds(o * 8 + part * 4, 4)],
                    vb.at[q, pl.ds(part * 4, 4), r, l],
                    5,
                    sem,
                    (dp, o),
                )

            each_in_plane(deal)
            keep(
                p1.at[q, pl.ds(mp * 8 + part * 4, 4)], vb.at[q, pl.ds(part * 4, 4), r, l], sem
            )
        ends.append((p1.at[q, pl.ds(0, 120)], snd.at[5]))

    def f4(q, part):
        await_bytes(vb.at[q, pl.ds(part * 4, 4)], s_fb.at[q * 2 + part])
        for k in range(part * 4, part * 4 + 4):
            if k:
                put(vb.at[q, k], gb.at[q, dp], 6, s_fc.at[q], (col(*COLUMN[k]), mp))
            else:
                keep(vb.at[q, k], gb.at[q, dp], s_fc.at[q])
        if part == FAR:
            ends.append((vb.at[q, pl.ds(0, 7)], snd.at[6]))

    def half_tile(q, lanes):
        rows = gb[q].reshape(8 * ROWS, W)
        value = jnp.dot(rows, rv[:, lanes], preferred_element_type=F32)
        half[:, pl.ds(q * ROWS, ROWS), lanes] = value.astype(BF).reshape(8, ROWS, TILE)

    def product_tile(q, lanes):
        rows = lv[:, pl.ds(q * ROWS, ROWS), :].reshape(8 * ROWS, W)
        value = jnp.dot(rows, half[:, :, lanes].reshape(W, TILE), preferred_element_type=F32)
        value = value.astype(BF)
        pp[q, :, :, lanes] = value.reshape(8, ROWS, TILE)
        wide = value.astype(F32)
        nrm[...] += fold(wide * wide)

    def by_tiles(body, q):
        def step(n, carry):
            body(q, pl.ds(pl.multiple_of(n * TILE, TILE), TILE))
            return carry

        lax.fori_loop(0, W // TILE, step, 0)

    def f5(q):
        loaded(rv, 1)
        await_bytes(gb.at[q], s_fc.at[q])
        by_tiles(half_tile, q)

    def product(q):
        by_tiles(product_tile, q)

    def give(q, ks, lanes):
        for k in ks:
            d = col(*COLUMN[k])
            sem = s_ra.at[q * 2 + k // 4]
            if k:
                put(pp.at[q, d, :, lanes], v2.at[q, k, :, lanes], 7, sem, (d, mp))
            else:
                keep(pp.at[q, d, :, lanes], v2.at[q, k, :, lanes], sem)

    def r0(q):
        give(q, range(8), pl.ds(0, W))
        ends.append((pp.at[q, pl.ds(0, 7)], snd.at[7]))

    def turn(q):
        loaded(lv, 2)
        await_bytes(gb.at[q], s_fc.at[q])
        first, second = pl.ds(0, TILE), pl.ds(TILE, TILE)
        half_tile(q, first)
        product_tile(0, first)
        give(0, range(6), first)
        half_tile(q, second)
        product_tile(0, second)
        give(0, range(4), second)
        give(0, (6, 7), first)
        give(0, range(4, 8), second)
        ends.append((pp.at[0, pl.ds(0, 7)], snd.at[7]))

    line0 = pl.ds(0, 1)

    def share_norm():
        total = jnp.full((1, 128), jnp.sum(nrm[...]), F32)
        nrm[0:1, :] = total
        nv[dp, 0:1, :] = total
        for dy, dc in COLUMN[1:]:
            put(nrm.at[line0], nv.at[dp, line0], 8, s_sm.at[1], (col(dy, dc), mp))
        ends.append((nv.at[pl.ds(0, 7), line0], snd.at[8]))

    def spread_norms():
        await_bytes(nv.at[pl.ds(0, 7), line0], s_sm.at[1])
        at = lax.broadcasted_iota(jnp.int32, (1, 128), 1)
        table = jnp.zeros((1, 128), F32)
        for s in range(8):
            table = jnp.where(at == s, nv[s, 0:1, :], table)
        nt[0:1, :] = table
        nw[mp, 0:1, :] = table

        def send(m):
            put(nt.at[line0], nw.at[mp, line0], 9, s_sm.at[2], (dp, m))

        each_in_plane(send)
        ends.append((nw.at[pl.ds(0, 15), line0], snd.at[9]))

    def r1(q, part):
        slots = pl.ds(part * 4, 4)
        await_bytes(v2.at[q, slots], s_ra.at[q * 2 + part])
        into = pl.ds(mp * 8 + part * 4, 4)

        def spread(m):
            r, l = piece(m)
            put(v2.at[q, slots, r, l], wb[q].at[into], 10, s_rb.at[q], (dp, m))

        each_in_plane(spread)
        r, l = piece(mp)
        keep(v2.at[q, slots, r, l], wb[q].at[into], s_rb.at[q])
        ends.append((wb[q].at[pl.ds(0, 60)], snd.at[10]))

    def r2(q):
        await_bytes(wb[q], s_rb.at[q])

        def pick(i, carry):
            for n in range(8):
                wp[q, i * 8 + n] = wb[q][inv[1, i * 8 + n]]
            return carry

        lax.fori_loop(0, 8, pick, 0)
        r, l = piece(mp)

        def deal(m):
            put(wp.at[q, pl.ds(m * 4, 4)], hh.at[q, :, r, l], 11, s_rc.at[q], (dp, m))

        each_in_plane(deal)
        keep(wp.at[q, pl.ds(mp * 4, 4)], hh.at[q, :, r, l], s_rc.at[q])
        ends.append((wp.at[q, pl.ds(0, 60)], snd.at[11]))

    def scales():
        await_bytes(ar.at[pl.ds(0, 7)], s_sm.at[0])
        await_bytes(nw.at[pl.ds(0, 15), line0], s_sm.at[2])
        loaded(momv, 3)
        at = lax.broadcasted_iota(jnp.int32, (1, 128), 1)
        sums = jnp.sum(ar[...], axis=0)
        for j in range(4):
            mine = nw[owner[mp * 4 + j], 0:1, :]
            pre = jnp.sum(jnp.where(at == slot[mp * 4 + j], mine, 0.0), axis=1, keepdims=True)
            scale = jnp.sqrt(sums[j : j + 1, :] / (pre + eps_norm))
            scl[j] = jnp.broadcast_to(scale, (8, 128))

    def rows_of(dy, q, first, count):
        return out_upd.at[pl.ds(first, count), col(dy, 0), pl.ds(q * ROWS, ROWS), :]

    def r3(q, first, count):
        if first == 0:
            await_bytes(hh.at[q], s_rc.at[q])
        for j in range(first, first + count):
            scale = jnp.concatenate([scl[j, 0:1, :]] * 8, axis=1)
            value = (
                beta_momentum * momv[j, pl.ds(q * ROWS, ROWS), :].astype(F32)
                + scale * hh[q, j].astype(F32)
            )
            up[q, j] = value.astype(BF)
        n = q * 2 + first // 2
        mine = up.at[q, pl.ds(first, count)]
        here = rows_of(0, q, first, count)
        put(mine, here, 12, s_a1.at[n * 2], up_dev)
        put(mine, here, 12, s_a1.at[n * 2 + 1], down_dev)
        put(mine, here, 14, s_sb.at[n * 4], sib_dev)
        keep(mine, here, s_out.at[4 + n])
        ends.extend([(here, snd.at[12]), (here, snd.at[12]), (here, snd.at[14])])
        ends.extend([(here, s_out.at[4 + n]), (here, s_sb.at[n * 4])])

    def r4(q, first, count):
        n = q * 2 + first // 2
        for k, dy in ((0, 3), (1, 1)):
            rows = rows_of(dy, q, first, count)
            await_bytes(rows, s_a1.at[n * 2 + k])
            part = rows_of(dy, q, first + k * (count // 2), count // 2)
            put(part, part, 13, s_a2.at[n * 2 + k], (up_dev, down_dev)[k])
            put(rows, rows, 14, s_sb.at[n * 4 + 1 + k], sib_dev)
            ends.extend([(part, snd.at[13]), (rows, snd.at[14]), (rows, s_sb.at[n * 4 + 1 + k])])

    def r5(q, first, count):
        n = q * 2 + first // 2
        for k in range(2):
            part = rows_of(2, q, first + k * (count // 2), count // 2)
            await_bytes(part, s_a2.at[n * 2 + k])
        rows = rows_of(2, q, first, count)
        put(rows, rows, 14, s_sb.at[n * 4 + 3], sib_dev)
        ends.extend([(rows, snd.at[14]), (rows, s_sb.at[n * 4 + 3])])

    swap(0)
    for stage, *which in (
        (f0, 0), (f0, 1), (f1, 0), (f1, 1), (f0, 2), (f0, 3), (f2, 0), (f2, 1), (f1, 2), (f3, 0),
        (f3, 1), (f1, 3), (f2, 2), (f4, 0, FAR), (f2, 3), (f4, 0, NEAR),
        (f4, 1, FAR), (f4, 1, NEAR), (f3, 2), (f4, 2, FAR), (f3, 3), (f5, 1), (f4, 2, NEAR),
        (f4, 3, FAR), (f5, 0), (f4, 3, NEAR), (share_adagrad,), (f5, 2),
        (turn, 3),
        (product, 1), (product, 2), (product, 3), (share_norm,), (r0, 1),
        (r0, 2), (r1, 0, NEAR), (r0, 3), (r1, 0, FAR), (r1, 1, NEAR), (spread_norms,), (r2, 0),
        (r1, 1, FAR), (scales,), (r3, 0, 0, 4), (r1, 2, FAR), (r2, 1), (r1, 2, NEAR),
        (r1, 3, FAR), (r3, 1, 0, 4), (r4, 0, 0, 4), (r2, 2), (r1, 3, NEAR), (r4, 1, 0, 4),
        (r3, 2, 0, 4), (r2, 3), (r3, 3, 0, 2), (r3, 3, 2, 2), (r4, 2, 0, 4), (r4, 3, 0, 2),
        (r5, 0, 0, 4), (r4, 3, 2, 2), (r5, 2, 0, 4), (r5, 1, 0, 4), (r5, 3, 0, 2), (r5, 3, 2, 2),
    ):
        stage(*which)

    for ref, sem in ends:
        await_bytes(ref, sem)


def store(acc, upd, out_acc, out_upd, sems):
    copies = []
    for j in range(4):
        copies.append(pltpu.make_async_copy(acc.at[j], out_acc.at[j], sems.at[j]))
        copies.append(pltpu.make_async_copy(upd.at[j], out_upd.at[j], sems.at[4 + j]))
    for copy in copies:
        copy.start()
    for copy in copies:
        copy.wait()


def shards(local_grads, left_root, right_root, accumulator, momentum, block_owner, block_slot):
    hbm = pl.BlockSpec(memory_space=pl.ANY)
    vmem = pl.BlockSpec(memory_space=pltpu.VMEM)
    smem = pl.BlockSpec(memory_space=pltpu.SMEM)
    V = pltpu.VMEM
    dma = pltpu.SemaphoreType.DMA
    C, R = CHUNKS, ROWS
    scratch = [
        V((C, 4, 4, R, W), BF), V((C, 4, 4, R, W), BF),
        V((C, 2, R, W), BF), V((C, 2, R, W), BF),
        V((C, 4, R, W), BF), V((C, 4, R, W), BF),
        V((4, 128, W), F32), V((4, 128, W), BF),
        V((8, 128, W), BF), V((W, W), BF),
        V((4, 8, 128), F32), V((8, 128), F32), V((8, 8, 128), F32),
        V((C, 4, R, W), BF),
        [V((64, 16, 128), BF)] * C, V((C, 128, 16, 128), BF),
        V((C, 8, R, W), BF), V((C, 8, R, W), BF),
        V((8, 128, W), BF), V((C, 8, R, W), BF),
        V((8, 128), F32), V((8, 8, 128), F32),
        V((8, 128), F32), V((16, 8, 128), F32),
        V((C, 8, R, W), BF),
        [V((128, 16, 128), BF)] * C, V((C, 64, 16, 128), BF),
        V((C, 4, R, W), BF), V((4, 8, 128), F32), V((C, 4, R, W), BF),
        V((8, 128), jnp.int32), pltpu.SMEM((8, 128), jnp.int32),
        dma((16,)), dma((5,)), dma((16,)), dma((8,)), dma((8,)),
        dma((4,)), dma((8,)), dma((4,)), dma((8,)), dma((4,)), dma((4,)),
        dma((3,)), dma((16,)), dma((16,)), dma((32,)), dma((12,)), dma((15,)),
    ]
    accum_new, update = pl.pallas_call(
        kernel,
        out_shape=(V((4, 128, W), F32), V((4, 8, 128, W), BF)),
        in_specs=[smem, smem] + [hbm] * 5,
        out_specs=(vmem, vmem),
        scratch_shapes=scratch,
        name="shampoo_step",
        compiler_params=pltpu.CompilerParams(
            collective_id=0, has_side_effects=True, vmem_limit_bytes=50 * 2**20
        ),
    )(
        block_owner,
        block_slot,
        local_grads.reshape(4, 4, 2, 128, W),
        left_root.reshape(8, 128, W),
        right_root.reshape(W, W),
        accumulator,
        momentum,
    )
    accum_new, update = pl.pallas_call(
        store,
        out_shape=(
            jax.ShapeDtypeStruct((4, 128, W), F32),
            jax.ShapeDtypeStruct((4, 8, 128, W), BF),
        ),
        in_specs=[vmem, vmem],
        out_specs=(hbm, hbm),
        scratch_shapes=[dma((8,))],
        name="store",
        compiler_params=pltpu.CompilerParams(vmem_limit_bytes=12 * 2**20),
    )(accum_new, update)
    return accum_new, update.reshape(4, W, W)


def solution(mesh):
    placed = (
        P("dp", "mp", None, None),
        P("mp", "dp", None, None),
        P("mp", "dp", None, None),
        P("mp", "dp", None),
        P("mp", "dp", None),
        P(),
        P(),
    )
    return jax.shard_map(
        shards,
        mesh=mesh,
        in_specs=placed,
        out_specs=(P("mp", "dp", None), P("mp", None, None)),
        check_vma=False,
    )
```

```python
import jax
import jax.numpy as jnp
from jax import lax
from jax.experimental import pallas as pl
from jax.experimental.pallas import tpu as pltpu
from jax.sharding import PartitionSpec as P

MESH = pl.DeviceIdType.MESH
BF = jnp.bfloat16
F32 = jnp.float32
beta_momentum = 0.9
eps_norm = 1e-06

CHUNKS = 4
TILE = 512
ROWS = 32
W = 1024
COLUMN = ((0, 0), (0, 1), (1, 1), (3, 1), (1, 0), (3, 0), (2, 0), (2, 1))
NEAR, FAR = 0, 1
PLANE = (
    (2, 2), (1, 2), (2, 1), (3, 2), (2, 3), (0, 2), (2, 0), (1, 1),
    (3, 3), (1, 3), (3, 1), (0, 1), (1, 0), (0, 3), (3, 0),
)


def kernel(
    owner, slot, g, left, right, acc, mom, out_acc, out_upd,
    own, sib, t1p, t1m, t2p, t2m, accv, momv, lv, rv, ada, adt, ar, sbuf, qb, p1, vb, gb, half, pp,
    nrm, nv, nt, nw, v2, wb, wp, hh, scl, up, invv, inv,
    s_own, s_in, s_sib, s_t1, s_t2, s_fa, s_fb, s_fc, s_ra, s_rb, s_rc, s_sm,
    s_a1, s_a2, s_sb, s_out, snd,
):
    dp = lax.axis_index("dp")
    mp = lax.axis_index("mp")
    y, c = dp // 2, dp % 2
    z, x = mp // 4, mp % 4
    piece_a, piece_h = mp // 8, mp % 8

    def col(dy, dc):
        return ((y + dy) % 4) * 2 + (c + dc) % 2

    def plane(dz, dx):
        return ((z + dz + c * (4 + dx - dz)) % 4) * 4 + (x + dx + c * (4 + dz - dx)) % 4

    def put(src, dst, ssem, rsem, device):
        pltpu.make_async_remote_copy(
            src_ref=src, dst_ref=dst, send_sem=snd.at[ssem], recv_sem=rsem,
            device_id=device, device_id_type=MESH,
        ).start()

    def keep(src, dst, sem):
        pltpu.make_async_copy(src, dst, sem).start()

    def await_bytes(ref, sem):
        pltpu.make_async_copy(ref, ref, sem).wait()

    seen_loads = set()

    def loaded(ref, n):
        if n not in seen_loads:
            seen_loads.add(n)
            await_bytes(ref, s_in.at[n])

    ends = []

    def place(b):
        return owner[b] * 8 + slot[b]

    def each_in_plane(body):
        for dz, dx in PLANE:
            body(plane(dz, dx))

    def piece(m):
        return pl.ds(pl.multiple_of((m // 8) * 16, 16), 16), pl.ds(
            pl.multiple_of((m % 8) * 128, 128), 128
        )

    up_dev = (col(1, 0), mp)
    down_dev = (col(3, 0), mp)
    sib_dev = (col(0, 1), mp)
    targets = ((y + 2) % 4, (y + 1) % 4, (y + 3) % 4, y)

    barrier = pltpu.get_barrier_semaphore()

    def greet(m):
        pl.semaphore_signal(barrier, inc=1, device_id=(dp, m), device_id_type=MESH)

    for dy, dc in COLUMN[1:]:
        pl.semaphore_signal(barrier, inc=1, device_id=(col(dy, dc), mp), device_id_type=MESH)
    each_in_plane(greet)
    for q in range(CHUNKS):
        for k in range(4):
            keep(
                g.at[:, targets[k], c, pl.ds(q * ROWS, ROWS), :],
                own.at[q, targets[k]],
                s_own.at[q * 4 + k],
            )
    lane = lax.broadcasted_iota(jnp.int32, (8, 128), 1)
    line = lax.broadcasted_iota(jnp.int32, (8, 128), 0)

    def fill(b, table):
        dy = (y + 4 - slot[b] // 2) % 4
        dc = (c + slot[b]) % 2
        across = jnp.where(dc == 1, 2 + dy // 2, 4 + dy // 2)
        seen = jnp.where(dy == 0, dc, jnp.where(dy == 2, 6 + dc, across))
        table = jnp.where((line == 0) & (lane == place(b)), b, table)
        return jnp.where((line == 1) & (lane == b), owner[b] * 8 + seen, table)

    invv[...] = lax.fori_loop(0, 64, fill, jnp.zeros((8, 128), jnp.int32))
    keep(invv, inv, s_in.at[4])
    keep(acc, accv, s_in.at[0])
    keep(right, rv, s_in.at[1])
    keep(left, lv, s_in.at[2])
    keep(mom, momv, s_in.at[3])

    pl.semaphore_wait(barrier, 22)

    def swap(q):
        for k in range(4):
            put(
                g.at[:, targets[k], 1 - c, pl.ds(q * ROWS, ROWS), :],
                sib.at[q, targets[k]],
                0,
                s_sib.at[q * 4 + k],
                sib_dev,
            )
            ends.append((sib.at[q, k], snd.at[0]))

    nrm[...] = jnp.zeros((8, 128), F32)
    for j in range(4):
        ada[j] = jnp.zeros((8, 128), F32)

    def both(q, k, j):
        t = targets[k]
        return own[q, t, j].astype(F32) + sib[q, t, j].astype(F32)

    def arrived(q, k):
        await_bytes(own.at[q, targets[k]], s_own.at[q * 4 + k])
        await_bytes(sib.at[q, targets[k]], s_sib.at[q * 4 + k])

    def fold(v):
        rows, lanes = v.shape
        v = jnp.sum(v.reshape(rows // 8, 8, lanes), axis=0)
        total = v[:, 0:128]
        for i in range(1, lanes // 128):
            total = total + v[:, i * 128 : (i + 1) * 128]
        return total

    def f0(q):
        if q + 1 < CHUNKS:
            swap(q + 1)
        arrived(q, 0)
        t = targets[0]
        for j in range(4):
            own[q, t, j] = both(q, 0, j).astype(BF)
        put(own.at[q, t, pl.ds(0, 2)], t1p.at[q], 1, s_t1.at[q * 2], up_dev)
        put(own.at[q, t, pl.ds(2, 2)], t1m.at[q], 1, s_t1.at[q * 2 + 1], down_dev)
        ends.extend([(t1p.at[q], snd.at[1]), (t1m.at[q], snd.at[1])])

    def f1(q):
        arrived(q, 1)
        arrived(q, 2)
        await_bytes(t1p.at[q], s_t1.at[q * 2])
        await_bytes(t1m.at[q], s_t1.at[q * 2 + 1])
        for j in range(4):
            value = both(q, 1, j)
            if j < 2:
                value = value + t1p[q, j].astype(F32)
            own[q, targets[1], j] = value.astype(BF)
        put(own.at[q, targets[1]], t2p.at[q], 2, s_t2.at[q * 2], up_dev)
        for j in range(4):
            value = both(q, 2, j)
            if j >= 2:
                value = value + t1m[q, j - 2].astype(F32)
            own[q, targets[2], j] = value.astype(BF)
        put(own.at[q, targets[2]], t2m.at[q], 2, s_t2.at[q * 2 + 1], down_dev)
        ends.extend([(t2p.at[q], snd.at[2]), (t2m.at[q], snd.at[2])])

    def f2(q):
        arrived(q, 3)
        await_bytes(t2p.at[q], s_t2.at[q * 2])
        await_bytes(t2m.at[q], s_t2.at[q * 2 + 1])
        loaded(accv, 0)
        rows = pl.ds(q * ROWS, ROWS)
        for j in range(4):
            total = both(q, 3, j) + t2p[q, j].astype(F32) + t2m[q, j].astype(F32)
            fresh = accv[j, rows, :] + total * total
            accv[j, rows, :] = fresh
            step = total * lax.rsqrt(fresh)
            ada[j] += fold(step * step)
            sbuf[q, j] = total.astype(BF)
        keep(accv.at[:, rows, :], out_acc.at[:, rows, :], s_out.at[q])

        def spread(m):
            r, l = piece(m)
            put(sbuf.at[q, :, r, l], qb[q].at[pl.ds(mp * 4, 4)], 3, s_fa.at[q], (dp, m))

        each_in_plane(spread)
        r, l = piece(mp)
        keep(sbuf.at[q, :, r, l], qb[q].at[pl.ds(mp * 4, 4)], s_fa.at[q])
        ends.extend([(qb[q].at[pl.ds(0, 60)], snd.at[3]), (out_acc.at[:, rows, :], s_out.at[q])])

    def share_adagrad():
        row = lax.broadcasted_iota(jnp.int32, (8, 128), 0)
        table = jnp.zeros((8, 128), F32)
        for j in range(4):
            table = jnp.where(row == j, jnp.sum(ada[j]), table)
        adt[...] = table
        ar[dp] = table
        for dy, dc in COLUMN[1:]:
            put(adt, ar.at[dp], 4, s_sm.at[0], (col(dy, dc), mp))
        ends.append((ar.at[pl.ds(0, 7)], snd.at[4]))

    def f3(q):
        loaded(inv, 4)
        await_bytes(qb[q], s_fa.at[q])

        def pick(o, carry):
            for n in range(8):
                p1[q, o * 8 + n] = qb[q][inv[0, o * 8 + col(*COLUMN[n])]]
            return carry

        lax.fori_loop(0, 16, pick, 0)
        r, l = piece(mp)
        for part in (FAR, NEAR):
            sem = s_fb.at[q * 2 + part]

            def deal(o):
                put(
                    p1.at[q, pl.ds(o * 8 + part * 4, 4)],
                    vb.at[q, pl.ds(part * 4, 4), r, l],
                    5,
                    sem,
                    (dp, o),
                )

            each_in_plane(deal)
            keep(
                p1.at[q, pl.ds(mp * 8 + part * 4, 4)], vb.at[q, pl.ds(part * 4, 4), r, l], sem
            )
        ends.append((p1.at[q, pl.ds(0, 120)], snd.at[5]))

    def f4(q, part):
        await_bytes(vb.at[q, pl.ds(part * 4, 4)], s_fb.at[q * 2 + part])
        for k in range(part * 4, part * 4 + 4):
            if k:
                put(vb.at[q, k], gb.at[q, dp], 6, s_fc.at[q], (col(*COLUMN[k]), mp))
            else:
                keep(vb.at[q, k], gb.at[q, dp], s_fc.at[q])
        if part == FAR:
            ends.append((vb.at[q, pl.ds(0, 7)], snd.at[6]))

    def half_tile(q, lanes):
        rows = gb[q].reshape(8 * ROWS, W)
        value = jnp.dot(rows, rv[:, lanes], preferred_element_type=F32)
        half[:, pl.ds(q * ROWS, ROWS), lanes] = value.astype(BF).reshape(8, ROWS, TILE)

    def product_tile(q, lanes):
        rows = lv[:, pl.ds(q * ROWS, ROWS), :].reshape(8 * ROWS, W)
        value = jnp.dot(rows, half[:, :, lanes].reshape(W, TILE), preferred_element_type=F32)
        value = value.astype(BF)
        pp[q, :, :, lanes] = value.reshape(8, ROWS, TILE)
        wide = value.astype(F32)
        nrm[...] += fold(wide * wide)

    def by_tiles(body, q):
        def step(n, carry):
            body(q, pl.ds(pl.multiple_of(n * TILE, TILE), TILE))
            return carry

        lax.fori_loop(0, W // TILE, step, 0)

    def f5(q):
        loaded(rv, 1)
        await_bytes(gb.at[q], s_fc.at[q])
        by_tiles(half_tile, q)

    def product(q):
        by_tiles(product_tile, q)

    def give(q, ks, lanes):
        for k in ks:
            d = col(*COLUMN[k])
            sem = s_ra.at[q * 2 + k // 4]
            if k:
                put(pp.at[q, d, :, lanes], v2.at[q, k, :, lanes], 7, sem, (d, mp))
            else:
                keep(pp.at[q, d, :, lanes], v2.at[q, k, :, lanes], sem)

    def r0(q):
        give(q, range(8), pl.ds(0, W))
        ends.append((pp.at[q, pl.ds(0, 7)], snd.at[7]))

    def turn(q):
        loaded(lv, 2)
        await_bytes(gb.at[q], s_fc.at[q])
        first, second = pl.ds(0, TILE), pl.ds(TILE, TILE)
        half_tile(q, first)
        product_tile(0, first)
        give(0, range(6), first)
        half_tile(q, second)
        product_tile(0, second)
        give(0, range(4), second)
        give(0, (6, 7), first)
        give(0, range(4, 8), second)
        ends.append((pp.at[0, pl.ds(0, 7)], snd.at[7]))

    line0 = pl.ds(0, 1)

    def share_norm():
        total = jnp.full((1, 128), jnp.sum(nrm[...]), F32)
        nrm[0:1, :] = total
        nv[dp, 0:1, :] = total
        for dy, dc in COLUMN[1:]:
            put(nrm.at[line0], nv.at[dp, line0], 8, s_sm.at[1], (col(dy, dc), mp))
        ends.append((nv.at[pl.ds(0, 7), line0], snd.at[8]))

    def spread_norms():
        await_bytes(nv.at[pl.ds(0, 7), line0], s_sm.at[1])
        at = lax.broadcasted_iota(jnp.int32, (1, 128), 1)
        table = jnp.zeros((1, 128), F32)
        for s in range(8):
            table = jnp.where(at == s, nv[s, 0:1, :], table)
        nt[0:1, :] = table
        nw[mp, 0:1, :] = table

        def send(m):
            put(nt.at[line0], nw.at[mp, line0], 9, s_sm.at[2], (dp, m))

        each_in_plane(send)
        ends.append((nw.at[pl.ds(0, 15), line0], snd.at[9]))

    def r1(q, part):
        slots = pl.ds(part * 4, 4)
        await_bytes(v2.at[q, slots], s_ra.at[q * 2 + part])
        into = pl.ds(mp * 8 + part * 4, 4)

        def spread(m):
            r, l = piece(m)
            put(v2.at[q, slots, r, l], wb[q].at[into], 10, s_rb.at[q], (dp, m))

        each_in_plane(spread)
        r, l = piece(mp)
        keep(v2.at[q, slots, r, l], wb[q].at[into], s_rb.at[q])
        ends.append((wb[q].at[pl.ds(0, 60)], snd.at[10]))

    def r2(q):
        await_bytes(wb[q], s_rb.at[q])

        def pick(i, carry):
            for n in range(8):
                wp[q, i * 8 + n] = wb[q][inv[1, i * 8 + n]]
            return carry

        lax.fori_loop(0, 8, pick, 0)
        r, l = piece(mp)

        def deal(m):
            put(wp.at[q, pl.ds(m * 4, 4)], hh.at[q, :, r, l], 11, s_rc.at[q], (dp, m))

        each_in_plane(deal)
        keep(wp.at[q, pl.ds(mp * 4, 4)], hh.at[q, :, r, l], s_rc.at[q])
        ends.append((wp.at[q, pl.ds(0, 60)], snd.at[11]))

    def scales():
        await_bytes(ar.at[pl.ds(0, 7)], s_sm.at[0])
        await_bytes(nw.at[pl.ds(0, 15), line0], s_sm.at[2])
        loaded(momv, 3)
        at = lax.broadcasted_iota(jnp.int32, (1, 128), 1)
        sums = jnp.sum(ar[...], axis=0)
        for j in range(4):
            mine = nw[owner[mp * 4 + j], 0:1, :]
            pre = jnp.sum(jnp.where(at == slot[mp * 4 + j], mine, 0.0), axis=1, keepdims=True)
            scale = jnp.sqrt(sums[j : j + 1, :] / (pre + eps_norm))
            scl[j] = jnp.broadcast_to(scale, (8, 128))

    def rows_of(dy, q, first, count):
        return out_upd.at[pl.ds(first, count), col(dy, 0), pl.ds(q * ROWS, ROWS), :]

    def r3(q, first, count):
        if first == 0:
            await_bytes(hh.at[q], s_rc.at[q])
        for j in range(first, first + count):
            scale = jnp.concatenate([scl[j, 0:1, :]] * 8, axis=1)
            value = (
                beta_momentum * momv[j, pl.ds(q * ROWS, ROWS), :].astype(F32)
                + scale * hh[q, j].astype(F32)
            )
            up[q, j] = value.astype(BF)
        n = q * 2 + first // 2
        mine = up.at[q, pl.ds(first, count)]
        here = rows_of(0, q, first, count)
        put(mine, here, 12, s_a1.at[n * 2], up_dev)
        put(mine, here, 12, s_a1.at[n * 2 + 1], down_dev)
        put(mine, here, 14, s_sb.at[n * 4], sib_dev)
        keep(mine, here, s_out.at[4 + n])
        ends.extend([(here, snd.at[12]), (here, snd.at[12]), (here, snd.at[14])])
        ends.extend([(here, s_out.at[4 + n]), (here, s_sb.at[n * 4])])

    def r4(q, first, count):
        n = q * 2 + first // 2
        for k, dy in ((0, 3), (1, 1)):
            rows = rows_of(dy, q, first, count)
            await_bytes(rows, s_a1.at[n * 2 + k])
            part = rows_of(dy, q, first + k * (count // 2), count // 2)
            put(part, part, 13, s_a2.at[n * 2 + k], (up_dev, down_dev)[k])
            put(rows, rows, 14, s_sb.at[n * 4 + 1 + k], sib_dev)
            ends.extend([(part, snd.at[13]), (rows, snd.at[14]), (rows, s_sb.at[n * 4 + 1 + k])])

    def r5(q, first, count):
        n = q * 2 + first // 2
        for k in range(2):
            part = rows_of(2, q, first + k * (count // 2), count // 2)
            await_bytes(part, s_a2.at[n * 2 + k])
        rows = rows_of(2, q, first, count)
        put(rows, rows, 14, s_sb.at[n * 4 + 3], sib_dev)
        ends.extend([(rows, snd.at[14]), (rows, s_sb.at[n * 4 + 3])])

    def settle(keep_last=0):
        early = ends[: len(ends) - keep_last]
        del ends[: len(early)]
        for ref, sem in early:
            await_bytes(ref, sem)

    swap(0)
    for stage, *which in (
        (f0, 0), (f0, 1), (f1, 0), (f1, 1), (f0, 2), (f0, 3), (f2, 0), (f2, 1), (f1, 2), (f3, 0),
        (f3, 1), (f1, 3), (f2, 2), (f4, 0, FAR), (f2, 3), (f4, 0, NEAR),
        (f4, 1, FAR), (f4, 1, NEAR), (f3, 2), (f4, 2, FAR), (f3, 3), (f5, 1), (f4, 2, NEAR),
        (f4, 3, FAR), (f5, 0), (f4, 3, NEAR), (share_adagrad,), (f5, 2),
        (turn, 3),
        (product, 1), (product, 2), (product, 3), (share_norm,), (r0, 1),
        (r0, 2), (r1, 0, NEAR), (r0, 3), (settle, 6), (r1, 0, FAR), (r1, 1, NEAR), (spread_norms,), (r2, 0),
        (r1, 1, FAR), (scales,), (r3, 0, 0, 4), (r1, 2, FAR), (r2, 1), (r1, 2, NEAR),
        (r1, 3, FAR), (r3, 1, 0, 4), (r4, 0, 0, 4), (r2, 2), (r1, 3, NEAR), (r4, 1, 0, 4),
        (r3, 2, 0, 4), (r2, 3), (r3, 3, 0, 2), (r3, 3, 2, 2), (settle, 45), (r4, 2, 0, 4), (r4, 3, 0, 2),
        (r5, 0, 0, 4), (r4, 3, 2, 2), (r5, 2, 0, 4), (r5, 1, 0, 4), (r5, 3, 0, 2), (r5, 3, 2, 2),
    ):
        stage(*which)

    for ref, sem in ends:
        await_bytes(ref, sem)


def store(acc, upd, out_acc, out_upd, sems):
    copies = []
    for j in range(4):
        copies.append(pltpu.make_async_copy(acc.at[j], out_acc.at[j], sems.at[j]))
        copies.append(pltpu.make_async_copy(upd.at[j], out_upd.at[j], sems.at[4 + j]))
    for copy in copies:
        copy.start()
    for copy in copies:
        copy.wait()


def shards(local_grads, left_root, right_root, accumulator, momentum, block_owner, block_slot):
    hbm = pl.BlockSpec(memory_space=pl.ANY)
    vmem = pl.BlockSpec(memory_space=pltpu.VMEM)
    smem = pl.BlockSpec(memory_space=pltpu.SMEM)
    V = pltpu.VMEM
    dma = pltpu.SemaphoreType.DMA
    C, R = CHUNKS, ROWS
    scratch = [
        V((C, 4, 4, R, W), BF), V((C, 4, 4, R, W), BF),
        V((C, 2, R, W), BF), V((C, 2, R, W), BF),
        V((C, 4, R, W), BF), V((C, 4, R, W), BF),
        V((4, 128, W), F32), V((4, 128, W), BF),
        V((8, 128, W), BF), V((W, W), BF),
        V((4, 8, 128), F32), V((8, 128), F32), V((8, 8, 128), F32),
        V((C, 4, R, W), BF),
        [V((64, 16, 128), BF)] * C, V((C, 128, 16, 128), BF),
        V((C, 8, R, W), BF), V((C, 8, R, W), BF),
        V((8, 128, W), BF), V((C, 8, R, W), BF),
        V((8, 128), F32), V((8, 8, 128), F32),
        V((8, 128), F32), V((16, 8, 128), F32),
        V((C, 8, R, W), BF),
        [V((128, 16, 128), BF)] * C, V((C, 64, 16, 128), BF),
        V((C, 4, R, W), BF), V((4, 8, 128), F32), V((C, 4, R, W), BF),
        V((8, 128), jnp.int32), pltpu.SMEM((8, 128), jnp.int32),
        dma((16,)), dma((5,)), dma((16,)), dma((8,)), dma((8,)),
        dma((4,)), dma((8,)), dma((4,)), dma((8,)), dma((4,)), dma((4,)),
        dma((3,)), dma((16,)), dma((16,)), dma((32,)), dma((12,)), dma((15,)),
    ]
    accum_new, update = pl.pallas_call(
        kernel,
        out_shape=(V((4, 128, W), F32), V((4, 8, 128, W), BF)),
        in_specs=[smem, smem] + [hbm] * 5,
        out_specs=(vmem, vmem),
        scratch_shapes=scratch,
        name="shampoo_step",
        compiler_params=pltpu.CompilerParams(
            collective_id=0, has_side_effects=True, vmem_limit_bytes=50 * 2**20
        ),
    )(
        block_owner,
        block_slot,
        local_grads.reshape(4, 4, 2, 128, W),
        left_root.reshape(8, 128, W),
        right_root.reshape(W, W),
        accumulator,
        momentum,
    )
    accum_new, update = pl.pallas_call(
        store,
        out_shape=(
            jax.ShapeDtypeStruct((4, 128, W), F32),
            jax.ShapeDtypeStruct((4, 8, 128, W), BF),
        ),
        in_specs=[vmem, vmem],
        out_specs=(hbm, hbm),
        scratch_shapes=[dma((8,))],
        name="store",
        compiler_params=pltpu.CompilerParams(vmem_limit_bytes=12 * 2**20),
    )(accum_new, update)
    return accum_new, update.reshape(4, W, W)


def solution(mesh):
    placed = (
        P("dp", "mp", None, None),
        P("mp", "dp", None, None),
        P("mp", "dp", None, None),
        P("mp", "dp", None),
        P("mp", "dp", None),
        P(),
        P(),
    )
    return jax.shard_map(
        shards,
        mesh=mesh,
        in_specs=placed,
        out_specs=(P("mp", "dp", None), P("mp", None, None)),
        check_vma=False,
    )
```
